256 devices in a mesh: cfg: 2 (over core), patch: 16 (over z, y_hi), tensor: 8 (over y_lo, x).
Axes of the slice: x: 4, y: 4 (y_hi: 2, y_lo: 2; y = y_hi * 2 + y_lo), z: 8, core: 2. Of those that a mesh axis runs over, the one named last changes fastest.
Arguments:
- hidden: bfloat16 [2, 2048, 3072], P('cfg', ('patch', 'tensor')), may hold values from -6 to 6
- stale_kv: bfloat16 [2, 2, 2048, 3072], P('cfg', None, 'patch', 'tensor'), may hold values from -80 to 80
- w_qkv: bfloat16 [3072, 3, 3072], P(None, None, 'tensor'), may hold values from -0.109375 to 0.109375
- w_out: bfloat16 [3072, 3072], P('tensor'), may hold values from -0.4375 to 0.4375
- mod_table: float32 [32, 3, 3072], replicated, may hold values from -5 to 5
- segment_ids: int32 [2048], replicated, may hold values from 0 to 7, never falling along the last dimension, each value on 1 to 1152 neighbouring positions
- step_index: int32 [8], replicated, may hold values from 0 to 31
- guide_scale: float32 [8], replicated, may hold values from 1.5 to 4
Outputs:
- branch_out: bfloat16 [2, 2048, 3072], P('cfg', ('patch', 'tensor'))
- guided: bfloat16 [2048, 3072], P(('patch', 'tensor'), 'cfg')
The draws below stay inside these ranges and needn't reach their ends.
Inputs may be any that keep to these rules, and one draw needn't show every extreme that they name: `segment_ids`: request ids never fall along the sequence; every request is present with 1 to 1152 tokens, one request exactly that many.
All inputs are finite; a program needn't handle non-finite values.
Results may differ from the reference program's by a relative error of at most 0.029.
Values may be sent and summed in bfloat16 or wider, within the bound.
A program may use at most 64 MiB of HBM per device.

```python
import math
import jax
import jax.numpy as jnp
import numpy as np
from jax import lax

D = 3072
HEADS = 24
HEAD_DIM = 128
TOK_DEV = 128
STEPS = 32
TOKENS = 2048
REQS = 8
N_PATCH = 16


def draw_stale_kv(key, part):
    key = jax.random.fold_in(key, 7)
    first_key = jax.random.fold_in(key, 1)
    shape = (2, 2, TOKENS, D)
    return jnp.clip(jax.random.normal(first_key, shape, jnp.float32), -6.0, 6.0).astype(jnp.bfloat16)


def place_ends(values, rng, smallest, top_value):
    place = [jax.random.randint(jax.random.fold_in(rng, axis), (), 0, length) for axis, length in enumerate(values.shape)]
    main_axis = values.shape.index(max(values.shape))
    next_to = place[:main_axis] + [(place[main_axis] + 1) % values.shape[main_axis]] + place[main_axis + 1:]
    return values.at[tuple(place)].set(smallest).at[tuple(next_to)].set(top_value)


def steps_of(own_key, shape, cuts, low, largest):
    def one(axis_at, parts):
        steps = jax.random.uniform(jax.random.fold_in(jax.random.fold_in(own_key, 6), axis_at), (parts,), jnp.float32, low / len(cuts), largest / len(cuts))
        return jnp.repeat(jnp.exp(steps), shape[axis_at] // parts).reshape((-1,) + (1,) * (len(shape) - axis_at - 1))

    gain = one(*cuts[0])
    for cut in cuts[1:]:
        gain = gain * one(*cut)
    return gain


def split_up(amount, total, limit, skew):
    loads = [(1 << 20) // math.isqrt(grade ** skew) + 1 for grade in range(2, amount + 1)]
    surplus, given = total - limit - (amount - 1), [1] * (amount - 1)
    while surplus > 0:
        candidates = [i for i in range(amount - 1) if given[i] < limit]
        pool, remaining = sum([loads[i] for i in candidates]), surplus
        for i in candidates:
            extra = min(limit - given[i], max(1, remaining * loads[i] // pool), surplus)
            given[i] = given[i] + extra
            surplus = surplus - extra
    return np.array([limit] + given)


def ragged_sizes(stream_key, amount, total, reach, lean):
    if amount == 2:
        one = jax.random.randint(stream_key, (), max(1, total - reach), min(reach, total - 1) + 1)
        return jnp.stack([one, total - one])
    tallies = jnp.asarray(split_up(amount, total, reach, lean), jnp.int32)
    pairs = (amount - 1) // 2
    source_of, receiver = tallies[1:1 + 2 * pairs:2], tallies[2:2 + 2 * pairs:2]
    margin = jnp.minimum(source_of - 1, reach - receiver)
    moved = jax.random.randint(jax.random.fold_in(stream_key, 1), (pairs,), 0, 1 << 20) % (margin + 1)
    tallies = tallies.at[1:1 + 2 * pairs:2].set(source_of - moved).at[2:2 + 2 * pairs:2].set(receiver + moved)
    return tallies[jax.random.permutation(jax.random.fold_in(stream_key, 2), amount)]


def centred(rng, shape, scale, bound, pieces=(), kind=jnp.bfloat16):
    entries = jax.random.normal(rng, shape, jnp.float32) * scale
    if len(pieces) > 0:
        entries = steps_of(rng, shape, pieces, -0.22, 0.18) * entries
    return jnp.clip(entries, min=-bound, max=bound).astype(kind)


def setup_inputs(seed: int = 0) -> dict:
    arg_keys = jax.random.split(jax.random.key(seed), 9)
    hidden = centred(arg_keys[0], (2, TOKENS, D), 1.0, 6.0, ((0, 2), (1, 128)))
    stale_kv = draw_stale_kv(jax.random.fold_in(arg_keys[8], 71), 0)
    w_qkv = centred(arg_keys[2], (D, 3, D), D ** -0.5, 0.109375, ((2, 8),))
    w_out = centred(arg_keys[3], (D, D), (D // 16) ** -0.5, 0.4375, ((0, 8),))
    mod_table = centred(arg_keys[4], (STEPS, 3, D), 1.0, 5.0, (), jnp.float32)
    segment_ids = jnp.searchsorted(jnp.cumsum(ragged_sizes(arg_keys[5], REQS, TOKENS, TOKENS // 2 + TOK_DEV, 0)), jnp.arange(TOKENS), side="right").astype(jnp.int32)
    step_index = place_ends(jax.random.randint(arg_keys[6], (REQS,), 0, STEPS), jax.random.fold_in(arg_keys[6], 1), 0, STEPS - 1).astype(jnp.int32)
    guide_scale = jnp.clip(jax.random.uniform(arg_keys[7], (REQS,), jnp.float32, 1.5, 4.0), 1.5, 4.0)
    return dict(hidden=hidden, stale_kv=stale_kv, w_qkv=w_qkv, w_out=w_out, mod_table=mod_table, segment_ids=segment_ids, step_index=step_index, guide_scale=guide_scale)


def reference(hidden, stale_kv, w_qkv, w_out, mod_table, segment_ids, step_index, guide_scale):
    request_mods = mod_table[step_index]
    token_mods = request_mods[segment_ids]
    shift_mod = token_mods[:, 0]
    scale_mod = token_mods[:, 1]
    gate_mod = token_mods[:, 2]
    residual_in = hidden.astype(jnp.float32)
    row_mean = lax.optimization_barrier(jnp.mean(residual_in, axis=-1, keepdims=True))
    row_var = lax.optimization_barrier(jnp.mean((residual_in - row_mean) ** 2, axis=-1, keepdims=True))
    normed = (residual_in - row_mean) / jnp.sqrt(row_var + 1e-06)
    modulated = (normed * (1.0 + scale_mod) + shift_mod).astype(jnp.bfloat16)
    fresh = jnp.dot(modulated.reshape(2 * TOKENS, D), w_qkv.reshape(D, 3 * D), preferred_element_type=jnp.float32).astype(jnp.bfloat16)
    fresh = fresh.reshape(2, TOKENS, 3, HEADS, HEAD_DIM)
    stale = stale_kv.reshape(2, 2, TOKENS, HEADS, HEAD_DIM)
    factor = 1.0 / HEAD_DIM ** 0.5
    outputs = []
    for branch in range(2):

        def slab_attention(slab_index):
            begin = (slab_index * TOK_DEV).astype(jnp.int32)
            queries = lax.dynamic_slice_in_dim(fresh[branch, :, 0], begin, TOK_DEV, 0)
            new_keys = lax.dynamic_slice_in_dim(fresh[branch, :, 1], begin, TOK_DEV, 0)
            new_vals = lax.dynamic_slice_in_dim(fresh[branch, :, 2], begin, TOK_DEV, 0)
            all_keys = lax.dynamic_update_slice_in_dim(stale[branch, 0], new_keys, begin, 0)
            all_vals = lax.dynamic_update_slice_in_dim(stale[branch, 1], new_vals, begin, 0)
            query_segs = lax.dynamic_slice_in_dim(segment_ids, begin, TOK_DEV, 0)
            allowed = query_segs[:, None] == segment_ids[None, :]
            scores = jnp.einsum('qhd,khd->hqk', queries.astype(jnp.float32), all_keys.astype(jnp.float32)) * factor
            scores = jnp.where(allowed[None], scores, -1e+30)
            row_max = lax.optimization_barrier(jnp.max(scores, axis=2, keepdims=True))
            weights = jnp.where(allowed[None], jnp.exp(scores - row_max), 0.0)
            row_sum = lax.optimization_barrier(jnp.sum(weights, axis=2))
            mixed = jnp.einsum('hqk,khd->hqd', weights.astype(jnp.bfloat16).astype(jnp.float32), all_vals.astype(jnp.float32))
            mixed = mixed / row_sum[..., None]
            return jnp.transpose(mixed, (1, 0, 2)).reshape(TOK_DEV, D).astype(jnp.bfloat16)
        slabs = lax.map(slab_attention, jnp.arange(N_PATCH, dtype=jnp.int32))
        outputs.append(slabs.reshape(TOKENS, D))
    attn = jnp.stack(outputs)
    projected = jnp.dot(attn.reshape(2 * TOKENS, D), w_out, preferred_element_type=jnp.float32).reshape(2, TOKENS, D)
    branch_out = (residual_in + gate_mod * projected).astype(jnp.bfloat16)
    strength = guide_scale[segment_ids][:, None]
    conditional = branch_out[0].astype(jnp.float32)
    unconditional = branch_out[1].astype(jnp.float32)
    guided = (unconditional + strength * (conditional - unconditional)).astype(jnp.bfloat16)
    return (branch_out, guided)
```

```python
import functools
import math

import jax
import jax.numpy as jnp
from jax import lax
from jax.experimental import pallas as pl
from jax.experimental.pallas import tpu as pltpu
from jax.sharding import PartitionSpec as P

MESH = pl.DeviceIdType.MESH
HEAD_DIM = 128
NZ = 8
NX = 4
NT = 8
NP = 16
KEY, VAL = 0, 1
NEG = -1e30


def slot_of(d, e):
    return (d % NZ) * 2 + e


FORWARD = {}
for _h in (KEY, VAL):
    FORWARD[(0, 0, _h)] = [("z+", -1, 0), ("z-", 1, 0), ("y", 0, 1)]
    FORWARD[(-1, 0, _h)] = [("z+", -2, 0), ("y", -1, 1)]
    FORWARD[(1, 0, _h)] = [("z-", 2, 0), ("y", 1, 1)]
    FORWARD[(-2, 0, _h)] = [("z+", -3, 0)]
    FORWARD[(2, 0, _h)] = [("z-", 3, 0)]
    FORWARD[(-3, 0, _h)] = [("y", -3, 1)]
    FORWARD[(3, 0, _h)] = [("y", 3, 1)]
    FORWARD[(-1, 1, _h)] = [("z+", -2, 1)]
    FORWARD[(1, 1, _h)] = [("z-", 2, 1)]
FORWARD[(-3, 0, KEY)].append(("z+", 4, 0))
FORWARD[(3, 0, VAL)].append(("z-", 4, 0))
FORWARD[(-3, 1, KEY)] = [("z+", 4, 1)]
FORWARD[(3, 1, VAL)] = [("z-", 4, 1)]
LINKS = {"z+": 0, "z-": 1, "y": 2}


def kernel(
    hidden,
    stale,
    w_qkv,
    w_out,
    mod_table,
    segments,
    steps,
    strengths,
    branch_out,
    guided_out,
    hid,
    mods,
    segs,
    query_segs,
    wq,
    wo,
    tokens,
    kv,
    queries,
    run_max,
    run_sum,
    mixed,
    attn,
    partial,
    parts,
    branch,
    partner,
    guided,
    local_sem,
    kv_send,
    kv_recv,
    tok_send,
    tok_recv,
    sum_send,
    sum_recv,
    pair_send,
    pair_recv,
    out_sem,
):
    cfg = lax.axis_index("cfg")
    patch = lax.axis_index("patch")
    tensor = lax.axis_index("tensor")
    z, yh = patch // 2, patch % 2
    yl, x = tensor // NX, tensor % NX
    width = hid.shape[1]
    half = width // 2
    rows = hid.shape[0]
    heads = queries.shape[1] // HEAD_DIM

    def tensor_peer(dx, dy):
        return (cfg, patch, ((yl + dy) % 2) * NX + (x + dx) % NX)

    links = {
        "z+": (cfg, ((z + 1) % NZ) * 2 + yh, tensor),
        "z-": (cfg, ((z + NZ - 1) % NZ) * 2 + yh, tensor),
        "y": (cfg, z * 2 + (1 - yh), tensor),
    }
    core = (1 - cfg, patch, tensor)
    peers = [(dx, dy) for dy in (0, 1) for dx in range(NX) if (dx, dy) != (0, 0)]

    loads = [
        pltpu.make_async_copy(hidden, hid, local_sem.at[0]),
        pltpu.make_async_copy(segments, segs, local_sem.at[1]),
        pltpu.make_async_copy(mod_table, mods, local_sem.at[2]),
        pltpu.make_async_copy(w_qkv, wq, local_sem.at[3]),
        pltpu.make_async_copy(w_out, wo, local_sem.at[4]),
    ]
    for load in loads:
        load.start()

    barrier = pltpu.get_barrier_semaphore()
    greeted = list(links.values()) + [core] + [tensor_peer(dx, dy) for dx, dy in peers]
    for device in greeted:
        pl.semaphore_signal(barrier, inc=1, device_id=device, device_id_type=MESH)

    loads[0].wait()
    residual = hid[...].astype(jnp.float32)
    mean = jnp.sum(residual, axis=-1, keepdims=True) * (1.0 / width)
    centred = residual - mean
    var = jnp.sum(centred * centred, axis=-1, keepdims=True) * (1.0 / width)
    normed = centred * lax.rsqrt(var + 1e-6)
    loads[1].wait()
    own_row = jnp.broadcast_to(segs[pl.ds(patch, 1), :], (NP * 8, NP * 8))
    query_segs[...] = own_row.T
    own_segs = query_segs[pl.ds(pl.multiple_of(tensor * rows, rows), rows), :]
    loads[2].wait()

    def token_mods(which):
        wide = jnp.concatenate([own_segs] * (width // 128), axis=1)
        picked = jnp.zeros((rows, width), jnp.float32)
        for r in range(8):
            row = mods[which, pl.ds(steps[r], 1), :]
            picked = jnp.where(wide == r, row, picked)
        return picked

    own_rows = pl.ds(pl.multiple_of(tensor * rows, rows), rows)
    tokens[own_rows, :] = (normed * (1.0 + token_mods(1)) + token_mods(0)).astype(jnp.bfloat16)

    pl.semaphore_wait(barrier, len(greeted))

    sent = []

    def send(src, dst, send_sem, recv_sem, device):
        copy = pltpu.make_async_remote_copy(
            src_ref=src,
            dst_ref=dst,
            send_sem=send_sem,
            recv_sem=recv_sem,
            device_id=device,
            device_id_type=MESH,
        )
        copy.start()
        sent.append(copy)

    def arrived(dst, recv_sem, send_sem):
        pltpu.make_async_remote_copy(
            src_ref=dst,
            dst_ref=dst,
            send_sem=send_sem,
            recv_sem=recv_sem,
            device_id=core,
            device_id_type=MESH,
        ).wait_recv()

    def token_rows(dx, dy):
        at = (((yl + dy) % 2) * NX + (x + dx) % NX) * rows
        return tokens.at[pl.ds(pl.multiple_of(at, rows), rows), :]

    def send_tokens(dy, dx_to, index):
        block = token_rows(0, dy)
        slot = dy * NX + (-dx_to) % NX
        send(block, block, tok_send.at[index], tok_recv.at[slot], tensor_peer(dx_to, 0))

    def wait_tokens(dx, dy):
        block = token_rows(dx, dy)
        arrived(block, tok_recv.at[dy * NX + dx], tok_send.at[0])

    counter = {"kv": 0}

    def spread(d, e, h):
        src = stale.at[h] if (d, e) == (0, 0) else kv.at[slot_of(d, e), h]
        for link, to_d, to_e in FORWARD.get((d, e, h), ()):
            slot = slot_of(to_d, to_e)
            send(
                src,
                kv.at[slot, h],
                kv_send.at[counter["kv"]],
                kv_recv.at[slot, h],
                links[link],
            )
            counter["kv"] += 1

    def take(d, e, h):
        slot = slot_of(d, e)
        arrived(kv.at[slot, h], kv_recv.at[slot, h], kv_send.at[0])
        spread(d, e, h)

    block = token_rows(0, 0)
    send(block, block, tok_send.at[0], tok_recv.at[NX], tensor_peer(0, 1))
    for index, dx in enumerate((1, NX - 1, 2)):
        send_tokens(0, dx, 1 + index)
    spread(0, 0, KEY)
    spread(0, 0, VAL)
    wait_tokens(0, 1)
    for index, dx in enumerate((1, NX - 1, 2)):
        send_tokens(1, dx, 4 + index)
    for h in (KEY, VAL):
        take(-1, 0, h)
        take(1, 0, h)
    for h in (KEY, VAL):
        take(-2, 0, h)
        take(2, 0, h)
        take(-1, 1, h)
        take(1, 1, h)
    for dx, dy in peers:
        if (dx, dy) != (0, 1):
            wait_tokens(dx, dy)
    loads[3].wait()
    for j in range(3):
        fresh = jnp.dot(tokens[...], wq[j], preferred_element_type=jnp.float32)
        fresh = fresh.astype(jnp.bfloat16)
        if j == 0:
            queries[...] = fresh
        else:
            kv[0, j - 1] = fresh

    scale = math.log2(math.e) / HEAD_DIM**0.5

    def attend(d, e, first=False):
        slot = slot_of(d, e)
        slab = ((z + d) % NZ) * 2 + (yh + e) % 2
        allowed = query_segs[...] == segs[pl.ds(slab, 1), :]
        for head in range(heads):
            cols = slice(head * HEAD_DIM, (head + 1) * HEAD_DIM)
            scores = lax.dot_general(
                queries[:, cols],
                kv[slot, KEY, :, cols],
                (((1,), (1,)), ((), ())),
                preferred_element_type=jnp.float32,
            )
            scores = jnp.where(allowed, scores * scale, NEG)
            top = jnp.max(scores, axis=1, keepdims=True)
            if first:
                new_max = jnp.broadcast_to(top, scores.shape)
            else:
                old_max = run_max[head]
                new_max = jnp.maximum(old_max, top)
            weights = jnp.exp2(scores - new_max)
            product = jnp.dot(
                weights.astype(jnp.bfloat16),
                kv[slot, VAL, :, cols],
                preferred_element_type=jnp.float32,
            )
            run_max[head] = new_max
            if first:
                run_sum[head] = weights
                mixed[head] = product
            else:
                shrink = jnp.exp2(old_max - new_max)
                run_sum[head] = run_sum[head] * shrink + weights
                mixed[head] = mixed[head] * shrink + product

    attend(0, 0, first=True)
    for h in (KEY, VAL):
        take(-3, 0, h)
        take(3, 0, h)
    attend(-1, 0)
    attend(1, 0)
    for h in (KEY, VAL):
        take(0, 1, h)
    attend(0, 1)
    attend(-2, 0)
    attend(2, 0)
    attend(-1, 1)
    attend(1, 1)
    for h in (KEY, VAL):
        take(-3, 1, h)
        take(3, 1, h)
    attend(-3, 0)
    attend(3, 0)
    for d, e in ((-2, 1), (2, 1), (4, 0)):
        for h in (KEY, VAL):
            take(d, e, h)
        attend(d, e)
    attend(-3, 1)
    attend(3, 1)
    for h in (KEY, VAL):
        take(4, 1, h)
    attend(4, 1)

    for head in range(heads):
        cols = slice(head * HEAD_DIM, (head + 1) * HEAD_DIM)
        total = jnp.sum(run_sum[head], axis=1, keepdims=True)
        attn[:, cols] = (mixed[head] / total).astype(jnp.bfloat16)

    loads[4].wait()
    for part in range(2):
        cols = slice(part * half, (part + 1) * half)
        partial[:, cols] = jnp.dot(
            attn[...], wo[:, cols], preferred_element_type=jnp.float32
        ).astype(jnp.bfloat16)
        for index, (dx, dy) in enumerate(peers):
            at = (((yl + dy) % 2) * NX + (x + dx) % NX) * rows
            back = peers.index(((-dx) % NX, dy))
            send(
                partial.at[pl.ds(pl.multiple_of(at, rows), rows), cols],
                parts.at[back, :, cols],
                sum_send.at[part, index],
                sum_recv.at[part, back],
                tensor_peer(dx, dy),
            )
    gate = token_mods(2)
    strength = jnp.zeros((rows, 128), jnp.float32)
    for r in range(8):
        strength = jnp.where(own_segs == r, strengths[r], strength)

    for part in range(2):
        cols = slice(part * half, (part + 1) * half)
        projected = partial[own_rows, cols].astype(jnp.float32)
        for index in range(len(peers)):
            arrived(parts.at[index, :, cols], sum_recv.at[part, index], sum_send.at[0, 0])
            projected = projected + parts[index, :, cols].astype(jnp.float32)
        branch[:, cols] = (
            hid[:, cols].astype(jnp.float32) + gate[:, cols] * projected
        ).astype(jnp.bfloat16)

    other_cols = pl.ds(pl.multiple_of((1 - cfg) * half, half), half)
    own_cols = pl.ds(pl.multiple_of(cfg * half, half), half)
    send(branch.at[:, other_cols], partner, pair_send, pair_recv, core)
    write = pltpu.make_async_copy(branch, branch_out, out_sem.at[0])
    write.start()
    arrived(partner, pair_recv, pair_send)
    mine = branch[:, own_cols].astype(jnp.float32)
    theirs = partner[...].astype(jnp.float32)
    first_branch = cfg == 0
    conditional = jnp.where(first_branch, mine, theirs)
    unconditional = jnp.where(first_branch, theirs, mine)
    wide = jnp.concatenate([strength] * (half // 128), axis=1)
    guided[...] = (unconditional + wide * (conditional - unconditional)).astype(jnp.bfloat16)
    last = pltpu.make_async_copy(guided, guided_out, out_sem.at[1])
    last.start()
    for copy in sent:
        copy.wait_send()
    write.wait()
    last.wait()


def body(hidden, stale_kv, w_qkv, w_out, mod_table, segment_ids, step_index, guide_scale):
    rows, width = hidden.shape[1:]
    slab = stale_kv.shape[2]
    local = w_qkv.shape[2]
    heads = local // HEAD_DIM
    bf16, f32 = jnp.bfloat16, jnp.float32
    anywhere = pl.BlockSpec(memory_space=pl.ANY)
    scalars = pl.BlockSpec(memory_space=pltpu.SMEM)
    dma = pltpu.SemaphoreType.DMA
    branch_rows, guided = pl.pallas_call(
        kernel,
        name="joint_attention",
        out_shape=(
            jax.ShapeDtypeStruct((rows, width), bf16),
            jax.ShapeDtypeStruct((rows, width // 2), bf16),
        ),
        in_specs=[anywhere] * 6 + [scalars] * 2,
        out_specs=(anywhere, anywhere),
        scratch_shapes=[
            pltpu.VMEM((rows, width), bf16),
            pltpu.VMEM((3, mod_table.shape[0], width), f32),
            pltpu.VMEM((NP, slab), jnp.int32),
            pltpu.VMEM((slab, slab), jnp.int32),
            pltpu.VMEM((3, width, local), bf16),
            pltpu.VMEM((local, width), bf16),
            pltpu.VMEM((slab, width), bf16),
            pltpu.VMEM((NP, 2, slab, local), bf16),
            pltpu.VMEM((slab, local), bf16),
            pltpu.VMEM((heads, slab, 128), f32),
            pltpu.VMEM((heads, slab, 128), f32),
            pltpu.VMEM((heads, slab, HEAD_DIM), f32),
            pltpu.VMEM((slab, local), bf16),
            pltpu.VMEM((slab, width), bf16),
            pltpu.VMEM((NT - 1, rows, width), bf16),
            pltpu.VMEM((rows, width), bf16),
            pltpu.VMEM((rows, width // 2), bf16),
            pltpu.VMEM((rows, width // 2), bf16),
            dma((5,)),
            dma((30,)),
            dma((NP, 2)),
            dma((7,)),
            dma((NT,)),
            dma((2, NT - 1)),
            dma((2, NT - 1)),
            dma,
            dma,
            dma((2,)),
        ],
        compiler_params=pltpu.CompilerParams(
            collective_id=0, has_side_effects=True, vmem_limit_bytes=62 << 20
        ),
    )(
        hidden[0],
        stale_kv[0],
        jnp.transpose(w_qkv, (1, 0, 2)),
        w_out,
        jnp.transpose(mod_table, (1, 0, 2)),
        segment_ids.reshape(NP, slab),
        step_index,
        guide_scale,
    )
    return branch_rows[None], guided


def solution(mesh):
    placed = (
        P("cfg", ("patch", "tensor"), None),
        P("cfg", None, "patch", "tensor"),
        P(None, None, "tensor"),
        P("tensor", None),
        P(),
        P(),
        P(),
        P(),
    )
    return jax.shard_map(
        body,
        mesh=mesh,
        in_specs=placed,
        out_specs=(P("cfg", ("patch", "tensor"), None), P(("patch", "tensor"), "cfg")),
        check_vma=False,
    )
```

```python
import functools
import math

import jax
import jax.numpy as jnp
from jax import lax
from jax.experimental import pallas as pl
from jax.experimental.pallas import tpu as pltpu
from jax.sharding import PartitionSpec as P

MESH = pl.DeviceIdType.MESH
HEAD_DIM = 128
NZ = 8
NX = 4
NT = 8
NP = 16
KEY, VAL = 0, 1
NEG = -1e30


CHUNKS = 4
LANES = 128


def kernel(
    hidden,
    stale,
    w_qkv,
    w_out,
    mod_table,
    segments,
    step_index,
    guide_scale,
    branch,
    guided,
    hid,
    mods,
    segs,
    steps,
    strengths,
    query_segs,
    wq,
    wo,
    tokens,
    kv,
    fresh_kv,
    queries,
    far_queries,
    bias,
    scores,
    mixed,
    far_mixed,
    far_back,
    stats,
    stats_back,
    attn,
    partial,
    parts,
    partner,
    local_sem,
    kv_send,
    kv_recv,
    tok_send,
    tok_recv,
    far_send,
    far_recv,
    sum_send,
    sum_recv,
    pair_send,
    pair_recv,
):
    cfg = lax.axis_index("cfg")
    patch = lax.axis_index("patch")
    tensor = lax.axis_index("tensor")
    z, yh = patch // 2, patch % 2
    yl, x = tensor // NX, tensor % NX
    rows, width = hid.shape
    half = width // 2
    slab = queries.shape[0]
    heads = queries.shape[1] // HEAD_DIM
    chunk = 2 * slab // CHUNKS

    def tensor_peer(dx, dy):
        return (cfg, patch, ((yl + dy) % 2) * NX + (x + dx) % NX)

    up = (cfg, ((z + 1) % NZ) * 2 + yh, tensor)
    down = (cfg, ((z + NZ - 1) % NZ) * 2 + yh, tensor)
    across = (cfg, z * 2 + (1 - yh), tensor)
    core = (1 - cfg, patch, tensor)
    peers = [(dx, dy) for dy in (0, 1) for dx in range(NX) if (dx, dy) != (0, 0)]

    loads = [
        pltpu.make_async_copy(hidden, hid, local_sem.at[0]),
        pltpu.make_async_copy(segments, segs, local_sem.at[1]),
        pltpu.make_async_copy(step_index, steps, local_sem.at[6]),
        pltpu.make_async_copy(guide_scale, strengths, local_sem.at[7]),
        pltpu.make_async_copy(mod_table, mods, local_sem.at[2]),
        pltpu.make_async_copy(w_qkv, wq, local_sem.at[3]),
        pltpu.make_async_copy(w_out, wo, local_sem.at[4]),
        pltpu.make_async_copy(stale, kv.at[0], local_sem.at[5]),
    ]
    for load in loads[:5]:
        load.start()

    barrier = pltpu.get_barrier_semaphore()
    greeted = [up, down, across, core] + [tensor_peer(dx, dy) for dx, dy in peers]
    for device in greeted:
        pl.semaphore_signal(barrier, inc=1, device_id=device, device_id_type=MESH)

    sent = []

    def send(src, dst, send_sem, recv_sem, device):
        copy = pltpu.make_async_remote_copy(
            src_ref=src,
            dst_ref=dst,
            send_sem=send_sem,
            recv_sem=recv_sem,
            device_id=device,
            device_id_type=MESH,
        )
        copy.start()
        sent.append(copy)

    def arrived(dst, recv_sem, send_sem):
        pltpu.make_async_remote_copy(
            src_ref=dst,
            dst_ref=dst,
            send_sem=send_sem,
            recv_sem=recv_sem,
            device_id=core,
            device_id_type=MESH,
        ).wait_recv()

    counter = [0]

    def block_of(ref, c):
        return ref.at[c // (CHUNKS // 2), pl.ds(c % (CHUNKS // 2) * chunk, chunk), :]

    def send_kv(src, d, c, device):
        send(
            src,
            block_of(kv.at[d % NZ], c),
            kv_send.at[counter[0]],
            kv_recv.at[d % NZ, c],
            device,
        )
        counter[0] += 1

    def take(d, c):
        here = block_of(kv.at[d % NZ], c)
        arrived(here, kv_recv.at[d % NZ, c], kv_send.at[0])
        if -3 < d < 0 or (d == -3 and c < CHUNKS // 2):
            send_kv(here, d - 1, c, up)
        if 0 < d < 3 or (d == 3 and c >= CHUNKS // 2):
            send_kv(here, d + 1, c, down)

    def token_rows(dx, dy):
        at = (((yl + dy) % 2) * NX + (x + dx) % NX) * rows
        return tokens.at[pl.ds(pl.multiple_of(at, rows), rows), :]

    def send_tokens(dy, dx_to, index):
        block = token_rows(0, dy)
        slot = dy * NX + (-dx_to) % NX
        send(block, block, tok_send.at[index], tok_recv.at[slot], tensor_peer(dx_to, 0))

    def wait_tokens(dx, dy):
        arrived(token_rows(dx, dy), tok_recv.at[dy * NX + dx], tok_send.at[0])

    loads[0].wait()
    residual = hid[...].astype(jnp.float32)
    mean = jnp.sum(residual, axis=-1, keepdims=True) * (1.0 / width)
    centred = residual - mean
    var = jnp.sum(centred * centred, axis=-1, keepdims=True) * (1.0 / width)
    normed = centred * lax.rsqrt(var + 1e-6)

    pl.semaphore_wait(barrier, len(greeted))
    for c in range(CHUNKS):
        send_kv(block_of(stale, c), -1, c, up)
        send_kv(block_of(stale, c), 1, c, down)

    def column(which):
        row = segs[pl.ds(which, 1), :]
        return jnp.broadcast_to(row, (slab, slab)).T

    loads[1].wait()
    query_segs[...] = column(patch)
    own_segs = query_segs[pl.ds(pl.multiple_of(tensor * rows, rows), rows), :]
    for load in loads[2:5]:
        load.wait()

    def token_mods(which):
        wide = jnp.concatenate([own_segs] * (width // LANES), axis=1)
        picked = jnp.zeros((rows, width), jnp.float32)
        for r in range(8):
            row = mods[which, pl.ds(steps[r], 1), :]
            picked = jnp.where(wide == r, row, picked)
        return picked

    own_rows = pl.ds(pl.multiple_of(tensor * rows, rows), rows)
    tokens[own_rows, :] = (normed * (1.0 + token_mods(1)) + token_mods(0)).astype(jnp.bfloat16)

    block = token_rows(0, 0)
    send(block, block, tok_send.at[0], tok_recv.at[NX], tensor_peer(0, 1))
    for index, dx in enumerate((1, NX - 1, 2)):
        send_tokens(0, dx, 1 + index)
    for load in loads[5:]:
        load.start()

    def fill_bias(which, seg_column):
        for d in range(NZ):
            key_row = segs[pl.ds(((z + d) % NZ) * 2 + yh, 1), :]
            bias[which, :, d * slab : (d + 1) * slab] = jnp.where(seg_column == key_row, 0.0, NEG)

    wait_tokens(0, 1)
    for index, dx in enumerate((1, NX - 1, 2)):
        send_tokens(1, dx, 4 + index)
    for c in range(CHUNKS):
        take(-1, c)
        take(1, c)
    fill_bias(0, query_segs[...])
    fill_bias(1, column(z * 2 + (1 - yh)))
    for c in range(CHUNKS):
        take(-2, c)
        take(2, c)
    for dx, dy in peers:
        if (dx, dy) != (0, 1):
            wait_tokens(dx, dy)
    loads[5].wait()
    queries[...] = jnp.dot(tokens[...], wq[0], preferred_element_type=jnp.float32).astype(
        jnp.bfloat16
    )
    send(queries, far_queries, far_send.at[0], far_recv.at[0], across)
    for c in range(CHUNKS):
        take(-3, c)
        take(3, c)
    for j in (KEY, VAL):
        fresh_kv[j] = jnp.dot(
            tokens[...], wq[1 + j], preferred_element_type=jnp.float32
        ).astype(jnp.bfloat16)

    scale = math.log2(math.e) / HEAD_DIM**0.5
    step = 2
    span = step * slab

    def score(which, q_ref, head):
        cols = slice(head * HEAD_DIM, (head + 1) * HEAD_DIM)
        top = None
        for i in range(NZ // step):
            keys = kv[i * step : (i + 1) * step, KEY, :, cols].reshape(span, HEAD_DIM)
            found = lax.dot_general(
                q_ref[:, cols], keys, (((1,), (1,)), ((), ())), preferred_element_type=jnp.float32
            )
            at = slice(i * span, (i + 1) * span)
            found = found * scale + bias[which, :, at]
            scores[head, :, at] = found
            for k in range(step):
                piece = found[:, k * slab : (k + 1) * slab]
                top = piece if top is None else jnp.maximum(top, piece)
        return jnp.max(top, axis=1, keepdims=True)

    def mix(head, top):
        cols = slice(head * HEAD_DIM, (head + 1) * HEAD_DIM)
        total, result = None, None
        for i in range(NZ // step):
            weights = jnp.exp2(scores[head, :, i * span : (i + 1) * span] - top)
            values = kv[i * step : (i + 1) * step, VAL, :, cols].reshape(span, HEAD_DIM)
            product = jnp.dot(
                weights.astype(jnp.bfloat16), values, preferred_element_type=jnp.float32
            )
            result = product if result is None else result + product
            for k in range(step):
                piece = weights[:, k * slab : (k + 1) * slab]
                total = piece if total is None else total + piece
        return jnp.sum(total, axis=1, keepdims=True), result

    arrived(far_queries, far_recv.at[0], far_send.at[0])
    loads[7].wait()
    for c in range(CHUNKS):
        take(4, c)
    lane = lax.broadcasted_iota(jnp.int32, (slab, LANES), 1)
    packed = jnp.zeros((slab, LANES), jnp.float32)
    tops = [score(1, far_queries, head) for head in range(heads)]
    for head in range(heads):
        total, result = mix(head, tops[head])
        far_mixed[head] = result.astype(jnp.bfloat16)
        send(
            far_mixed.at[head],
            far_back.at[head],
            far_send.at[1 + head],
            far_recv.at[1 + head],
            across,
        )
        packed = jnp.where(lane == head, tops[head], packed)
        packed = jnp.where(lane == heads + head, total, packed)
    stats[...] = packed.T[:8]
    send(stats, stats_back, far_send.at[1 + heads], far_recv.at[1 + heads], across)

    for j in (KEY, VAL):
        kv[0, j] = fresh_kv[j]
    tops = [score(0, queries, head) for head in range(heads)]
    own = [mix(head, tops[head]) for head in range(heads)]
    for head in range(heads):
        mixed[head] = own[head][1]

    arrived(stats_back, far_recv.at[1 + heads], far_send.at[0])
    back = jnp.concatenate([stats_back[...]] * (LANES // 8), axis=0).T
    for head in range(heads):
        cols = slice(head * HEAD_DIM, (head + 1) * HEAD_DIM)
        far_top, far_total = back[:, head : head + 1], back[:, heads + head : heads + head + 1]
        top = jnp.maximum(tops[head], far_top)
        near_part, far_part = jnp.exp2(tops[head] - top), jnp.exp2(far_top - top)
        total = own[head][0] * near_part + far_total * far_part
        arrived(far_back.at[head], far_recv.at[1 + head], far_send.at[0])
        result = mixed[head] * near_part + far_back[head].astype(jnp.float32) * far_part
        attn[:, cols] = (result / total).astype(jnp.bfloat16)

    loads[6].wait()
    for part in range(2):
        cols = slice(part * half, (part + 1) * half)
        partial[:, cols] = jnp.dot(
            attn[...], wo[:, cols], preferred_element_type=jnp.float32
        ).astype(jnp.bfloat16)
        for index, (dx, dy) in enumerate(peers):
            at = (((yl + dy) % 2) * NX + (x + dx) % NX) * rows
            slot = peers.index(((-dx) % NX, dy))
            send(
                partial.at[pl.ds(pl.multiple_of(at, rows), rows), cols],
                parts.at[slot, :, cols],
                sum_send.at[part, index],
                sum_recv.at[part, slot],
                tensor_peer(dx, dy),
            )
    gate = token_mods(2)
    strength = jnp.zeros((rows, LANES), jnp.float32)
    for r in range(8):
        strength = jnp.where(own_segs == r, strengths[r], strength)

    for part in range(2):
        cols = slice(part * half, (part + 1) * half)
        projected = partial[own_rows, cols].astype(jnp.float32)
        for index in range(len(peers)):
            arrived(parts.at[index, :, cols], sum_recv.at[part, index], sum_send.at[0, 0])
            projected = projected + parts[index, :, cols].astype(jnp.float32)
        branch[:, cols] = (
            hid[:, cols].astype(jnp.float32) + gate[:, cols] * projected
        ).astype(jnp.bfloat16)

    other_cols = pl.ds(pl.multiple_of((1 - cfg) * half, half), half)
    own_cols = pl.ds(pl.multiple_of(cfg * half, half), half)
    send(branch.at[:, other_cols], partner, pair_send, pair_recv, core)
    arrived(partner, pair_recv, pair_send)
    mine = branch[:, own_cols].astype(jnp.float32)
    theirs = partner[...].astype(jnp.float32)
    first_branch = cfg == 0
    conditional = jnp.where(first_branch, mine, theirs)
    unconditional = jnp.where(first_branch, theirs, mine)
    wide = jnp.concatenate([strength] * (half // LANES), axis=1)
    guided[...] = (unconditional + wide * (conditional - unconditional)).astype(jnp.bfloat16)
    for copy in sent:
        copy.wait_send()


def body(hidden, stale_kv, w_qkv, w_out, mod_table, segment_ids, step_index, guide_scale):
    rows, width = hidden.shape[1:]
    slab = stale_kv.shape[2]
    local = w_qkv.shape[2]
    heads = local // HEAD_DIM
    bf16, f32 = jnp.bfloat16, jnp.float32
    anywhere = pl.BlockSpec(memory_space=pl.ANY)
    dma = pltpu.SemaphoreType.DMA
    def pinned(array):
        return pltpu.with_memory_space_constraint(array, pltpu.HBM)

    branch_rows, guided = pl.pallas_call(
        kernel,
        name="joint_attention",
        out_shape=(
            pltpu.VMEM((rows, width), bf16),
            pltpu.VMEM((rows, width // 2), bf16),
        ),
        in_specs=[anywhere] * 8,
        out_specs=(
            pl.BlockSpec(memory_space=pltpu.VMEM),
            pl.BlockSpec(memory_space=pltpu.VMEM),
        ),
        scratch_shapes=[
            pltpu.VMEM((rows, width), bf16),
            pltpu.VMEM((3, mod_table.shape[0], width), f32),
            pltpu.VMEM((NP, slab), jnp.int32),
            pltpu.SMEM(step_index.shape, jnp.int32),
            pltpu.SMEM(guide_scale.shape, f32),
            pltpu.VMEM((slab, slab), jnp.int32),
            pltpu.VMEM((3, width, local), bf16),
            pltpu.VMEM((local, width), bf16),
            pltpu.VMEM((slab, width), bf16),
            pltpu.VMEM((NZ, 2, slab, local), bf16),
            pltpu.VMEM((2, slab, local), bf16),
            pltpu.VMEM((slab, local), bf16),
            pltpu.VMEM((slab, local), bf16),
            pltpu.VMEM((2, slab, NZ * slab), f32),
            pltpu.VMEM((heads, slab, NZ * slab), f32),
            pltpu.VMEM((heads, slab, HEAD_DIM), f32),
            pltpu.VMEM((heads, slab, HEAD_DIM), bf16),
            pltpu.VMEM((heads, slab, HEAD_DIM), bf16),
            pltpu.VMEM((8, LANES), f32),
            pltpu.VMEM((8, LANES), f32),
            pltpu.VMEM((slab, local), bf16),
            pltpu.VMEM((slab, width), bf16),
            pltpu.VMEM((NT - 1, rows, width), bf16),
            pltpu.VMEM((rows, width // 2), bf16),
            dma((8,)),
            dma((7 * CHUNKS,)),
            dma((NZ, CHUNKS)),
            dma((7,)),
            dma((NT,)),
            dma((2 + heads,)),
            dma((2 + heads,)),
            dma((2, NT - 1)),
            dma((2, NT - 1)),
            dma,
            dma,
        ],
        compiler_params=pltpu.CompilerParams(
            collective_id=0, has_side_effects=True, vmem_limit_bytes=48 << 20
        ),
    )(
        pinned(hidden[0]),
        pinned(stale_kv[0]),
        pinned(jnp.transpose(w_qkv, (1, 0, 2))),
        pinned(w_out),
        pinned(jnp.transpose(mod_table, (1, 0, 2))),
        pinned(segment_ids.reshape(NP, slab)),
        pinned(step_index),
        pinned(guide_scale),
    )
    return branch_rows[None], guided


def solution(mesh):
    placed = (
        P("cfg", ("patch", "tensor"), None),
        P("cfg", None, "patch", "tensor"),
        P(None, None, "tensor"),
        P("tensor", None),
        P(),
        P(),
        P(),
        P(),
    )
    return jax.shard_map(
        body,
        mesh=mesh,
        in_specs=placed,
        out_specs=(P("cfg", ("patch", "tensor"), None), P(("patch", "tensor"), "cfg")),
        check_vma=False,
    )
```

```python
import functools
import math

import jax
import jax.numpy as jnp
from jax import lax
from jax.experimental import pallas as pl
from jax.experimental.pallas import tpu as pltpu
from jax.sharding import PartitionSpec as P

MESH = pl.DeviceIdType.MESH
HEAD_DIM = 128
NZ = 8
NX = 4
NT = 8
NP = 16
KEY, VAL = 0, 1
NEG = -1e30


PARTS = 1
CHUNKS = 4
LANES = 128


def kernel(
    hidden,
    stale,
    w_qkv,
    w_out,
    mod_table,
    segments,
    step_index,
    guide_scale,
    branch,
    guided,
    hid,
    mods,
    segs,
    steps,
    strengths,
    query_segs,
    wq,
    wo,
    tokens,
    kv,
    fresh_kv,
    queries,
    far_queries,
    bias,
    scores,
    far_mixed,
    far_back,
    stats,
    stats_back,
    attn,
    partial,
    hops,
    onward,
    parts,
    partner,
    local_sem,
    kv_send,
    kv_recv,
    tok_send,
    tok_recv,
    far_send,
    far_recv,
    sum_send,
    sum_recv,
    pair_send,
    pair_recv,
):
    cfg = lax.axis_index("cfg")
    patch = lax.axis_index("patch")
    tensor = lax.axis_index("tensor")
    z, yh = patch // 2, patch % 2
    yl, x = tensor // NX, tensor % NX
    rows, width = hid.shape
    half = width // 2
    slab = queries.shape[0]
    heads = queries.shape[1] // HEAD_DIM
    chunk = 2 * slab // CHUNKS

    def tensor_peer(dx, dy):
        return (cfg, patch, ((yl + dy) % 2) * NX + (x + dx) % NX)

    up = (cfg, ((z + 1) % NZ) * 2 + yh, tensor)
    down = (cfg, ((z + NZ - 1) % NZ) * 2 + yh, tensor)
    across = (cfg, z * 2 + (1 - yh), tensor)
    core = (1 - cfg, patch, tensor)

    barrier = pltpu.get_barrier_semaphore()
    greeted = [up, down, across, core] + [tensor_peer(*to) for to in ((1, 0), (NX - 1, 0), (2, 0), (0, 1))]
    for device in greeted:
        pl.semaphore_signal(barrier, inc=1, device_id=device, device_id_type=MESH)

    loads = [
        pltpu.make_async_copy(hidden, hid, local_sem.at[0]),
        pltpu.make_async_copy(segments, segs, local_sem.at[1]),
        pltpu.make_async_copy(step_index, steps, local_sem.at[6]),
        pltpu.make_async_copy(guide_scale, strengths, local_sem.at[7]),
        pltpu.make_async_copy(mod_table, mods, local_sem.at[2]),
        pltpu.make_async_copy(w_qkv, wq, local_sem.at[3]),
        pltpu.make_async_copy(w_out, wo, local_sem.at[4]),
        pltpu.make_async_copy(stale, kv.at[0], local_sem.at[5]),
    ]
    for load in loads[:5]:
        load.start()

    sent = []

    def send(src, dst, send_sem, recv_sem, device):
        copy = pltpu.make_async_remote_copy(
            src_ref=src,
            dst_ref=dst,
            send_sem=send_sem,
            recv_sem=recv_sem,
            device_id=device,
            device_id_type=MESH,
        )
        copy.start()
        sent.append(copy)

    def arrived(dst, recv_sem, send_sem):
        pltpu.make_async_remote_copy(
            src_ref=dst,
            dst_ref=dst,
            send_sem=send_sem,
            recv_sem=recv_sem,
            device_id=core,
            device_id_type=MESH,
        ).wait_recv()

    counter = [0]

    def swap(c):
        return (c + CHUNKS // 2) % CHUNKS

    def block_of(ref, c):
        return ref.at[c // (CHUNKS // 2), pl.ds(c % (CHUNKS // 2) * chunk, chunk), :]

    def send_kv(src, d, c, device):
        send(
            src,
            block_of(kv.at[d % NZ], c),
            kv_send.at[counter[0]],
            kv_recv.at[d % NZ, c],
            device,
        )
        counter[0] += 1

    def take(d, c):
        here = block_of(kv.at[d % NZ], c)
        arrived(here, kv_recv.at[d % NZ, c], kv_send.at[0])
        if -3 < d < 0 or (d == -3 and c < CHUNKS // 2):
            send_kv(here, d - 1, c, up)
        if 0 < d < 3 or (d == 3 and c >= CHUNKS // 2):
            send_kv(here, d + 1, c, down)

    def token_block(dx, dy, part):
        at = (((yl + dy) % 2) * NX + (x + dx) % NX) * rows
        return tokens.at[pl.ds(pl.multiple_of(at, rows), rows), part * half : (part + 1) * half]

    def send_tokens(dx, dy, to_dx, to_dy, index, part):
        block = token_block(dx, dy, part)
        slot = ((dy + to_dy) % 2) * NX + (dx - to_dx) % NX
        send(
            block,
            block,
            tok_send.at[part, index],
            tok_recv.at[part, slot],
            tensor_peer(to_dx, to_dy),
        )

    def wait_tokens(dx, dy, part):
        arrived(token_block(dx, dy, part), tok_recv.at[part, dy * NX + dx], tok_send.at[0, 0])

    def relay_tokens(part):
        for index, dx in enumerate((1, NX - 1)):
            wait_tokens(dx, 0, part)
            send_tokens(dx, 0, 0, 1, 4 + index, part)
        wait_tokens(0, 1, part)
        send_tokens(0, 1, 2, 0, 6, part)

    pl.semaphore_wait(barrier, len(greeted))
    for c in range(CHUNKS):
        send_kv(block_of(stale, c), -1, c, up)
        send_kv(block_of(stale, swap(c)), 1, swap(c), down)

    loads[0].wait()
    residual = hid[...].astype(jnp.float32)
    mean = jnp.sum(residual, axis=-1, keepdims=True) * (1.0 / width)
    centred = residual - mean
    var = jnp.sum(centred * centred, axis=-1, keepdims=True) * (1.0 / width)
    normed = centred * lax.rsqrt(var + 1e-6)

    def column(which):
        row = segs[pl.ds(which, 1), :]
        return jnp.broadcast_to(row, (slab, slab)).T

    loads[1].wait()
    query_segs[...] = column(patch)
    own_segs = query_segs[pl.ds(pl.multiple_of(tensor * rows, rows), rows), :]
    for load in loads[2:5]:
        load.wait()

    def token_mods(which, start, count):
        wide = jnp.concatenate([own_segs] * (count // LANES), axis=1)
        picked = jnp.zeros((rows, count), jnp.float32)
        for r in range(8):
            row = mods[which, pl.ds(steps[r], 1), pl.ds(start, count)]
            picked = jnp.where(wide == r, row, picked)
        return picked

    own_rows = pl.ds(pl.multiple_of(tensor * rows, rows), rows)
    shift, scale = token_mods(0, 0, width), token_mods(1, 0, width)
    tokens[own_rows, :] = (normed * (1.0 + scale) + shift).astype(jnp.bfloat16)

    for part in range(2):
        send_tokens(0, 0, 1, 0, 0, part)
        send_tokens(0, 0, NX - 1, 0, 1, part)
        send_tokens(0, 0, 0, 1, 2, part)
    for part in range(2):
        send_tokens(0, 0, 2, 0, 3, part)
    for load in loads[5:]:
        load.start()

    def fill_bias(which, seg_column):
        for d in range(NZ):
            key_row = segs[pl.ds(((z + d) % NZ) * 2 + yh, 1), :]
            bias[which, :, d * slab : (d + 1) * slab] = jnp.where(seg_column == key_row, 0.0, NEG)

    def take_both(d, c):
        take(-d, c)
        take(d, swap(c))

    for part in range(2):
        relay_tokens(part)
        for c in range(part * CHUNKS // 2, (part + 1) * CHUNKS // 2):
            take_both(1, c)
    fill_bias(0, query_segs[...])
    fill_bias(1, column(z * 2 + (1 - yh)))
    for c in range(CHUNKS):
        take_both(2, c)
    for part in range(2):
        for dx, dy in ((2, 0), (1, 1), (NX - 1, 1), (2, 1)):
            wait_tokens(dx, dy, part)
    loads[5].wait()
    queries[...] = jnp.dot(tokens[...], wq[0], preferred_element_type=jnp.float32).astype(
        jnp.bfloat16
    )
    send(queries, far_queries, far_send.at[0], far_recv.at[0], across)
    for c in range(CHUNKS):
        take_both(3, c)
    for j in (KEY, VAL):
        fresh_kv[j] = jnp.dot(
            tokens[...], wq[1 + j], preferred_element_type=jnp.float32
        ).astype(jnp.bfloat16)

    scale = math.log2(math.e) / HEAD_DIM**0.5

    def meet(which, q_ref, runs):
        cols = [slice(head * HEAD_DIM, (head + 1) * HEAD_DIM) for head in range(heads)]
        tops = []
        for head in range(heads):
            top = None
            for first, count in runs:
                at = slice(first * slab, (first + count) * slab)
                keys = kv[first : first + count, KEY, :, cols[head]].reshape(count * slab, HEAD_DIM)
                found = lax.dot_general(
                    q_ref[:, cols[head]],
                    keys,
                    (((1,), (1,)), ((), ())),
                    preferred_element_type=jnp.float32,
                )
                found = found * scale + bias[which, :, at]
                scores[head, :, at] = found
                for k in range(count):
                    piece = found[:, k * slab : (k + 1) * slab]
                    top = piece if top is None else jnp.maximum(top, piece)
            tops.append(jnp.max(top, axis=1, keepdims=True))
        met = []
        for head in range(heads):
            total, result = None, None
            for first, count in runs:
                at = slice(first * slab, (first + count) * slab)
                weights = jnp.exp2(scores[head, :, at] - tops[head])
                values = kv[first : first + count, VAL, :, cols[head]].reshape(
                    count * slab, HEAD_DIM
                )
                product = jnp.dot(
                    weights.astype(jnp.bfloat16), values, preferred_element_type=jnp.float32
                )
                result = product if result is None else result + product
                for k in range(count):
                    piece = weights[:, k * slab : (k + 1) * slab]
                    total = piece if total is None else total + piece
            met.append((tops[head], jnp.sum(total, axis=1, keepdims=True), result))
        return met

    def merge(one, two):
        top = jnp.maximum(one[0], two[0])
        left, right = jnp.exp2(one[0] - top), jnp.exp2(two[0] - top)
        return top, one[1] * left + two[1] * right, one[2] * left + two[2] * right

    early, late = ((0, 2), (2, 2), (5, 3)), ((4, 1),)

    arrived(far_queries, far_recv.at[0], far_send.at[0])
    loads[7].wait()
    far = meet(1, far_queries, early)
    for j in (KEY, VAL):
        kv[0, j] = fresh_kv[j]
    own = meet(0, queries, early)
    for c in range(CHUNKS // 2):
        take(4, c)
        take(4, swap(c))
    lane = lax.broadcasted_iota(jnp.int32, (slab, LANES), 1)
    packed = jnp.zeros((slab, LANES), jnp.float32)
    far_late = meet(1, far_queries, late)
    for head in range(heads):
        top, total, result = merge(far[head], far_late[head])
        far_mixed[head] = result.astype(jnp.bfloat16)
        send(
            far_mixed.at[head],
            far_back.at[head],
            far_send.at[1 + head],
            far_recv.at[1 + head],
            across,
        )
        packed = jnp.where(lane == head, top, packed)
        packed = jnp.where(lane == heads + head, total, packed)
    stats[...] = packed.T[:8]
    send(stats, stats_back, far_send.at[1 + heads], far_recv.at[1 + heads], across)
    own_late = meet(0, queries, late)
    own = [merge(own[head], own_late[head]) for head in range(heads)]

    arrived(stats_back, far_recv.at[1 + heads], far_send.at[0])
    back = jnp.concatenate([stats_back[...]] * (LANES // 8), axis=0).T
    for head in range(heads):
        cols = slice(head * HEAD_DIM, (head + 1) * HEAD_DIM)
        arrived(far_back.at[head], far_recv.at[1 + head], far_send.at[0])
        top, total, result = merge(
            own[head],
            (
                back[:, head : head + 1],
                back[:, heads + head : heads + head + 1],
                far_back[head].astype(jnp.float32),
            ),
        )
        attn[:, cols] = (result / total).astype(jnp.bfloat16)

    piece = half // PARTS
    starts = [
        pl.multiple_of(which * half + part * piece, piece)
        for which in (1 - cfg, cfg)
        for part in range(PARTS)
    ]
    loads[6].wait()

    def sum_rows(dx, dy):
        at = (((yl + dy) % 2) * NX + (x + dx) % NX) * rows
        return pl.ds(pl.multiple_of(at, rows), rows)

    for part in range(2 * PARTS):
        partial[part] = jnp.dot(
            attn[...], wo[:, pl.ds(starts[part], piece)], preferred_element_type=jnp.float32
        ).astype(jnp.bfloat16)
        for index, (row, to, landing) in enumerate(
            (
                (sum_rows(1, 1), tensor_peer(0, 1), hops.at[part, 0]),
                (sum_rows(NX - 1, 1), tensor_peer(0, 1), hops.at[part, 1]),
                (sum_rows(2, 1), tensor_peer(2, 0), hops.at[part, 2]),
                (sum_rows(2, 0), tensor_peer(2, 0), parts.at[part, 2]),
            )
        ):
            send(
                partial.at[part, row, :],
                landing,
                sum_send.at[part, index],
                sum_recv.at[part, index],
                to,
            )
    strength = jnp.zeros((rows, LANES), jnp.float32)
    for r in range(8):
        strength = jnp.where(own_segs == r, strengths[r], strength)
    gates = [token_mods(2, start, piece) for start in starts]

    for part in range(2 * PARTS):
        for index, (row, to, slot) in enumerate(
            (
                (sum_rows(1, 0), tensor_peer(1, 0), 0),
                (sum_rows(NX - 1, 0), tensor_peer(NX - 1, 0), 1),
                (sum_rows(0, 1), tensor_peer(0, 1), 3),
            )
        ):
            arrived(hops.at[part, index], sum_recv.at[part, index], sum_send.at[0, 0])
            both = hops[part, index].astype(jnp.float32) + partial[part, row, :].astype(jnp.float32)
            onward[part, index] = both.astype(jnp.bfloat16)
            send(
                onward.at[part, index],
                parts.at[part, slot],
                sum_send.at[part, 4 + index],
                sum_recv.at[part, 4 + index],
                to,
            )

    sums = []
    for part in range(2 * PARTS):
        cols = pl.ds(starts[part], piece)
        projected = partial[part, own_rows, :].astype(jnp.float32)
        for slot, sem in ((2, 3), (0, 4), (1, 5), (3, 6)):
            arrived(parts.at[part, slot], sum_recv.at[part, sem], sum_send.at[0, 0])
            projected = projected + parts[part, slot].astype(jnp.float32)
        total = hid[:, cols].astype(jnp.float32) + gates[part] * projected
        sums.append(total.astype(jnp.bfloat16))
        branch[:, cols] = sums[part]
        if part < PARTS:
            send(branch.at[:, cols], partner.at[part], pair_send.at[part], pair_recv.at[part], core)

    first_branch = cfg == 0
    wide = jnp.concatenate([strength] * (piece // LANES), axis=1)
    for part in range(PARTS):
        arrived(partner.at[part], pair_recv.at[part], pair_send.at[0])
        mine = sums[PARTS + part].astype(jnp.float32)
        theirs = partner[part].astype(jnp.float32)
        conditional = jnp.where(first_branch, mine, theirs)
        unconditional = jnp.where(first_branch, theirs, mine)
        guided[:, part * piece : (part + 1) * piece] = (
            unconditional + wide * (conditional - unconditional)
        ).astype(jnp.bfloat16)
    for copy in sent:
        copy.wait_send()


def body(hidden, stale_kv, w_qkv, w_out, mod_table, segment_ids, step_index, guide_scale):
    rows, width = hidden.shape[1:]
    slab = stale_kv.shape[2]
    local = w_qkv.shape[2]
    heads = local // HEAD_DIM
    piece = width // 2 // PARTS
    bf16, f32 = jnp.bfloat16, jnp.float32
    anywhere = pl.BlockSpec(memory_space=pl.ANY)
    dma = pltpu.SemaphoreType.DMA
    def pinned(array):
        return pltpu.with_memory_space_constraint(array, pltpu.HBM)

    branch_rows, guided = pl.pallas_call(
        kernel,
        name="joint_attention",
        out_shape=(
            pltpu.VMEM((rows, width), bf16),
            pltpu.VMEM((rows, width // 2), bf16),
        ),
        in_specs=[anywhere] * 8,
        out_specs=(
            pl.BlockSpec(memory_space=pltpu.VMEM),
            pl.BlockSpec(memory_space=pltpu.VMEM),
        ),
        scratch_shapes=[
            pltpu.VMEM((rows, width), bf16),
            pltpu.VMEM((3, mod_table.shape[0], width), f32),
            pltpu.VMEM((NP, slab), jnp.int32),
            pltpu.SMEM(step_index.shape, jnp.int32),
            pltpu.SMEM(guide_scale.shape, f32),
            pltpu.VMEM((slab, slab), jnp.int32),
            pltpu.VMEM((3, width, local), bf16),
            pltpu.VMEM((local, width), bf16),
            pltpu.VMEM((slab, width), bf16),
            pltpu.VMEM((NZ, 2, slab, local), bf16),
            pltpu.VMEM((2, slab, local), bf16),
            pltpu.VMEM((slab, local), bf16),
            pltpu.VMEM((slab, local), bf16),
            pltpu.VMEM((2, slab, NZ * slab), f32),
            pltpu.VMEM((heads, slab, NZ * slab), f32),
            pltpu.VMEM((heads, slab, HEAD_DIM), bf16),
            pltpu.VMEM((heads, slab, HEAD_DIM), bf16),
            pltpu.VMEM((8, LANES), f32),
            pltpu.VMEM((8, LANES), f32),
            pltpu.VMEM((slab, local), bf16),
            pltpu.VMEM((2 * PARTS, slab, piece), bf16),
            pltpu.VMEM((2 * PARTS, 3, rows, piece), bf16),
            pltpu.VMEM((2 * PARTS, 3, rows, piece), bf16),
            pltpu.VMEM((2 * PARTS, 4, rows, piece), bf16),
            pltpu.VMEM((PARTS, rows, piece), bf16),
            dma((8,)),
            dma((7 * CHUNKS,)),
            dma((NZ, CHUNKS)),
            dma((2, 7)),
            dma((2, NT)),
            dma((2 + heads,)),
            dma((2 + heads,)),
            dma((2 * PARTS, NT - 1)),
            dma((2 * PARTS, NT - 1)),
            dma((PARTS,)),
            dma((PARTS,)),
        ],
        compiler_params=pltpu.CompilerParams(
            collective_id=0, has_side_effects=True, vmem_limit_bytes=48 << 20
        ),
    )(
        pinned(hidden[0]),
        pinned(stale_kv[0]),
        pinned(jnp.transpose(w_qkv, (1, 0, 2))),
        pinned(w_out),
        pinned(jnp.transpose(mod_table, (1, 0, 2))),
        pinned(segment_ids.reshape(NP, slab)),
        pinned(step_index),
        pinned(guide_scale),
    )
    return branch_rows[None], guided


def solution(mesh):
    placed = (
        P("cfg", ("patch", "tensor"), None),
        P("cfg", None, "patch", "tensor"),
        P(None, None, "tensor"),
        P("tensor", None),
        P(),
        P(),
        P(),
        P(),
    )
    return jax.shard_map(
        body,
        mesh=mesh,
        in_specs=placed,
        out_specs=(P("cfg", ("patch", "tensor"), None), P(("patch", "tensor"), "cfg")),
        check_vma=False,
    )
```

```python
import functools
import math

import jax
import jax.numpy as jnp
from jax import lax
from jax.experimental import pallas as pl
from jax.experimental.pallas import tpu as pltpu
from jax.sharding import PartitionSpec as P

MESH = pl.DeviceIdType.MESH
HEAD_DIM = 128
NZ = 8
NX = 4
NT = 8
NP = 16
KEY, VAL = 0, 1
NEG = -1e30


PARTS = 1
CHUNKS = 4
LANES = 128


def kernel(
    hidden,
    stale,
    w_qkv,
    w_out,
    mod_table,
    segments,
    step_index,
    guide_scale,
    branch,
    guided,
    hid,
    mods,
    segs,
    steps,
    strengths,
    query_segs,
    wq,
    wo,
    tokens,
    kv,
    fresh_kv,
    queries,
    far_queries,
    bias,
    scores,
    far_mixed,
    far_back,
    stats,
    stats_back,
    attn,
    partial,
    hops,
    onward,
    parts,
    partner,
    local_sem,
    kv_send,
    kv_recv,
    tok_send,
    tok_recv,
    far_send,
    far_recv,
    sum_send,
    sum_recv,
    pair_send,
    pair_recv,
):
    cfg = lax.axis_index("cfg")
    patch = lax.axis_index("patch")
    tensor = lax.axis_index("tensor")
    z, yh = patch // 2, patch % 2
    yl, x = tensor // NX, tensor % NX
    rows, width = hid.shape
    half = width // 2
    slab = queries.shape[0]
    heads = queries.shape[1] // HEAD_DIM
    chunk = 2 * slab // CHUNKS

    def tensor_peer(dx, dy):
        return (cfg, patch, ((yl + dy) % 2) * NX + (x + dx) % NX)

    up = (cfg, ((z + 1) % NZ) * 2 + yh, tensor)
    down = (cfg, ((z + NZ - 1) % NZ) * 2 + yh, tensor)
    across = (cfg, z * 2 + (1 - yh), tensor)
    core = (1 - cfg, patch, tensor)

    barrier = pltpu.get_barrier_semaphore()
    greeted = [up, down, across, core] + [tensor_peer(*to) for to in ((1, 0), (NX - 1, 0), (2, 0), (0, 1))]
    for device in greeted:
        pl.semaphore_signal(barrier, inc=1, device_id=device, device_id_type=MESH)

    loads = [
        pltpu.make_async_copy(hidden, hid, local_sem.at[0]),
        pltpu.make_async_copy(segments, segs, local_sem.at[1]),
        pltpu.make_async_copy(step_index, steps, local_sem.at[6]),
        pltpu.make_async_copy(guide_scale, strengths, local_sem.at[7]),
        pltpu.make_async_copy(mod_table, mods, local_sem.at[2]),
        pltpu.make_async_copy(w_qkv, wq, local_sem.at[3]),
        pltpu.make_async_copy(w_out, wo, local_sem.at[4]),
        pltpu.make_async_copy(stale, kv.at[0], local_sem.at[5]),
    ]
    for load in loads[:5]:
        load.start()

    sent = []

    def send(src, dst, send_sem, recv_sem, device):
        copy = pltpu.make_async_remote_copy(
            src_ref=src,
            dst_ref=dst,
            send_sem=send_sem,
            recv_sem=recv_sem,
            device_id=device,
            device_id_type=MESH,
        )
        copy.start()
        sent.append(copy)

    def arrived(dst, recv_sem, send_sem):
        pltpu.make_async_remote_copy(
            src_ref=dst,
            dst_ref=dst,
            send_sem=send_sem,
            recv_sem=recv_sem,
            device_id=core,
            device_id_type=MESH,
        ).wait_recv()

    counter = [0]

    def swap(c):
        return (c + CHUNKS // 2) % CHUNKS

    def block_of(ref, c):
        return ref.at[c // (CHUNKS // 2), pl.ds(c % (CHUNKS // 2) * chunk, chunk), :]

    def send_kv(src, d, c, device):
        send(
            src,
            block_of(kv.at[d % NZ], c),
            kv_send.at[counter[0]],
            kv_recv.at[d % NZ, c],
            device,
        )
        counter[0] += 1

    def take(d, c):
        here = block_of(kv.at[d % NZ], c)
        arrived(here, kv_recv.at[d % NZ, c], kv_send.at[0])
        if -3 < d < 0 or (d == -3 and c < CHUNKS // 2):
            send_kv(here, d - 1, c, up)
        if 0 < d < 3 or (d == 3 and c >= CHUNKS // 2):
            send_kv(here, d + 1, c, down)

    def token_block(dx, dy, part):
        at = (((yl + dy) % 2) * NX + (x + dx) % NX) * rows
        return tokens.at[pl.ds(pl.multiple_of(at, rows), rows), part * half : (part + 1) * half]

    def send_tokens(dx, dy, to_dx, to_dy, index, part):
        block = token_block(dx, dy, part)
        slot = ((dy + to_dy) % 2) * NX + (dx - to_dx) % NX
        send(
            block,
            block,
            tok_send.at[part, index],
            tok_recv.at[part, slot],
            tensor_peer(to_dx, to_dy),
        )

    def wait_tokens(dx, dy, part):
        arrived(token_block(dx, dy, part), tok_recv.at[part, dy * NX + dx], tok_send.at[0, 0])

    def relay_tokens(part):
        for index, dx in enumerate((1, NX - 1)):
            wait_tokens(dx, 0, part)
            send_tokens(dx, 0, 0, 1, 4 + index, part)
        wait_tokens(0, 1, part)
        send_tokens(0, 1, 2, 0, 6, part)

    pl.semaphore_wait(barrier, len(greeted))
    for c in range(CHUNKS):
        send_kv(block_of(stale, c), -1, c, up)
        send_kv(block_of(stale, swap(c)), 1, swap(c), down)

    loads[0].wait()
    residual = hid[...].astype(jnp.float32)
    mean = jnp.sum(residual, axis=-1, keepdims=True) * (1.0 / width)
    centred = residual - mean
    var = jnp.sum(centred * centred, axis=-1, keepdims=True) * (1.0 / width)
    normed = centred * lax.rsqrt(var + 1e-6)

    def column(which):
        row = segs[pl.ds(which, 1), :]
        return jnp.broadcast_to(row, (slab, slab)).T

    loads[1].wait()
    query_segs[...] = column(patch)
    own_segs = query_segs[pl.ds(pl.multiple_of(tensor * rows, rows), rows), :]
    for load in loads[2:5]:
        load.wait()

    def token_mods(which, start, count):
        wide = jnp.concatenate([own_segs] * (count // LANES), axis=1)
        picked = jnp.zeros((rows, count), jnp.float32)
        for r in range(8):
            row = mods[which, pl.ds(steps[r], 1), pl.ds(start, count)]
            picked = jnp.where(wide == r, row, picked)
        return picked

    own_rows = pl.ds(pl.multiple_of(tensor * rows, rows), rows)
    shift, scale = token_mods(0, 0, width), token_mods(1, 0, width)
    tokens[own_rows, :] = (normed * (1.0 + scale) + shift).astype(jnp.bfloat16)

    for part in range(2):
        send_tokens(0, 0, 1, 0, 0, part)
        send_tokens(0, 0, NX - 1, 0, 1, part)
        send_tokens(0, 0, 0, 1, 2, part)
    for part in range(2):
        send_tokens(0, 0, 2, 0, 3, part)
    for load in loads[5:]:
        load.start()

    def fill_bias(which, seg_column):
        for d in range(NZ):
            key_row = segs[pl.ds(((z + d) % NZ) * 2 + yh, 1), :]
            bias[which, :, d * slab : (d + 1) * slab] = jnp.where(seg_column == key_row, 0.0, NEG)

    def take_both(d, c):
        take(-d, c)
        take(d, swap(c))

    for c in range(CHUNKS // 2):
        take_both(1, c)
    relay_tokens(0)
    relay_tokens(1)
    for c in range(CHUNKS // 2, CHUNKS):
        take_both(1, c)
    fill_bias(0, query_segs[...])
    fill_bias(1, column(z * 2 + (1 - yh)))
    for c in range(CHUNKS):
        take_both(2, c)
    for part in range(2):
        for dx, dy in ((2, 0), (1, 1), (NX - 1, 1), (2, 1)):
            wait_tokens(dx, dy, part)
    loads[5].wait()
    queries[...] = jnp.dot(tokens[...], wq[0], preferred_element_type=jnp.float32).astype(
        jnp.bfloat16
    )
    send(queries, far_queries, far_send.at[0], far_recv.at[0], across)
    for c in range(CHUNKS):
        take_both(3, c)
    for j in (KEY, VAL):
        fresh_kv[j] = jnp.dot(
            tokens[...], wq[1 + j], preferred_element_type=jnp.float32
        ).astype(jnp.bfloat16)

    scale = math.log2(math.e) / HEAD_DIM**0.5

    def meet(which, q_ref, runs):
        cols = [slice(head * HEAD_DIM, (head + 1) * HEAD_DIM) for head in range(heads)]
        tops = []
        for head in range(heads):
            top = None
            for first, count in runs:
                at = slice(first * slab, (first + count) * slab)
                keys = kv[first : first + count, KEY, :, cols[head]].reshape(count * slab, HEAD_DIM)
                found = lax.dot_general(
                    q_ref[:, cols[head]],
                    keys,
                    (((1,), (1,)), ((), ())),
                    preferred_element_type=jnp.float32,
                )
                found = found * scale + bias[which, :, at]
                scores[head, :, at] = found
                for k in range(count):
                    piece = found[:, k * slab : (k + 1) * slab]
                    top = piece if top is None else jnp.maximum(top, piece)
            tops.append(jnp.max(top, axis=1, keepdims=True))
        met = []
        for head in range(heads):
            total, result = None, None
            for first, count in runs:
                at = slice(first * slab, (first + count) * slab)
                weights = jnp.exp2(scores[head, :, at] - tops[head])
                values = kv[first : first + count, VAL, :, cols[head]].reshape(
                    count * slab, HEAD_DIM
                )
                product = jnp.dot(
                    weights.astype(jnp.bfloat16), values, preferred_element_type=jnp.float32
                )
                result = product if result is None else result + product
                for k in range(count):
                    piece = weights[:, k * slab : (k + 1) * slab]
                    total = piece if total is None else total + piece
            met.append((tops[head], jnp.sum(total, axis=1, keepdims=True), result))
        return met

    def merge(one, two):
        top = jnp.maximum(one[0], two[0])
        left, right = jnp.exp2(one[0] - top), jnp.exp2(two[0] - top)
        return top, one[1] * left + two[1] * right, one[2] * left + two[2] * right

    early, late = ((0, 2), (2, 2), (5, 3)), ((4, 1),)

    arrived(far_queries, far_recv.at[0], far_send.at[0])
    loads[7].wait()
    far = meet(1, far_queries, early)
    for j in (KEY, VAL):
        kv[0, j] = fresh_kv[j]
    own = meet(0, queries, early)
    for c in range(CHUNKS // 2):
        take(4, c)
        take(4, swap(c))
    lane = lax.broadcasted_iota(jnp.int32, (slab, LANES), 1)
    packed = jnp.zeros((slab, LANES), jnp.float32)
    far_late = meet(1, far_queries, late)
    for head in range(heads):
        top, total, result = merge(far[head], far_late[head])
        far_mixed[head] = result.astype(jnp.bfloat16)
        send(
            far_mixed.at[head],
            far_back.at[head],
            far_send.at[1 + head],
            far_recv.at[1 + head],
            across,
        )
        packed = jnp.where(lane == head, top, packed)
        packed = jnp.where(lane == heads + head, total, packed)
    stats[...] = packed.T[:8]
    send(stats, stats_back, far_send.at[1 + heads], far_recv.at[1 + heads], across)
    own_late = meet(0, queries, late)
    own = [merge(own[head], own_late[head]) for head in range(heads)]

    arrived(stats_back, far_recv.at[1 + heads], far_send.at[0])
    back = jnp.concatenate([stats_back[...]] * (LANES // 8), axis=0).T
    for head in range(heads):
        cols = slice(head * HEAD_DIM, (head + 1) * HEAD_DIM)
        arrived(far_back.at[head], far_recv.at[1 + head], far_send.at[0])
        top, total, result = merge(
            own[head],
            (
                back[:, head : head + 1],
                back[:, heads + head : heads + head + 1],
                far_back[head].astype(jnp.float32),
            ),
        )
        attn[:, cols] = (result / total).astype(jnp.bfloat16)

    piece = half // PARTS
    starts = [
        pl.multiple_of(which * half + part * piece, piece)
        for which in (1 - cfg, cfg)
        for part in range(PARTS)
    ]
    loads[6].wait()

    def sum_rows(dx, dy):
        at = (((yl + dy) % 2) * NX + (x + dx) % NX) * rows
        return pl.ds(pl.multiple_of(at, rows), rows)

    for part in range(2 * PARTS):
        partial[part] = jnp.dot(
            attn[...], wo[:, pl.ds(starts[part], piece)], preferred_element_type=jnp.float32
        ).astype(jnp.bfloat16)
        for index, (row, to, landing) in enumerate(
            (
                (sum_rows(1, 1), tensor_peer(0, 1), hops.at[part, 0]),
                (sum_rows(NX - 1, 1), tensor_peer(0, 1), hops.at[part, 1]),
                (sum_rows(2, 1), tensor_peer(2, 0), hops.at[part, 2]),
                (sum_rows(2, 0), tensor_peer(2, 0), parts.at[part, 2]),
            )
        ):
            send(
                partial.at[part, row, :],
                landing,
                sum_send.at[part, index],
                sum_recv.at[part, index],
                to,
            )
    for copy in sent[:-8 * PARTS]:
        copy.wait_send()
    del sent[: -8 * PARTS]
    strength = jnp.zeros((rows, LANES), jnp.float32)
    for r in range(8):
        strength = jnp.where(own_segs == r, strengths[r], strength)
    gates = [token_mods(2, start, piece) for start in starts]

    for part in range(2 * PARTS):
        for index, (row, to, slot) in enumerate(
            (
                (sum_rows(1, 0), tensor_peer(1, 0), 0),
                (sum_rows(NX - 1, 0), tensor_peer(NX - 1, 0), 1),
                (sum_rows(0, 1), tensor_peer(0, 1), 3),
            )
        ):
            arrived(hops.at[part, index], sum_recv.at[part, index], sum_send.at[0, 0])
            both = hops[part, index].astype(jnp.float32) + partial[part, row, :].astype(jnp.float32)
            onward[part, index] = both.astype(jnp.bfloat16)
            send(
                onward.at[part, index],
                parts.at[part, slot],
                sum_send.at[part, 4 + index],
                sum_recv.at[part, 4 + index],
                to,
            )

    sums = []
    for part in range(2 * PARTS):
        cols = pl.ds(starts[part], piece)
        projected = partial[part, own_rows, :].astype(jnp.float32)
        for slot, sem in ((2, 3), (0, 4), (1, 5), (3, 6)):
            arrived(parts.at[part, slot], sum_recv.at[part, sem], sum_send.at[0, 0])
            projected = projected + parts[part, slot].astype(jnp.float32)
        total = hid[:, cols].astype(jnp.float32) + gates[part] * projected
        sums.append(total.astype(jnp.bfloat16))
        branch[:, cols] = sums[part]
        if part < PARTS:
            send(branch.at[:, cols], partner.at[part], pair_send.at[part], pair_recv.at[part], core)

    first_branch = cfg == 0
    wide = jnp.concatenate([strength] * (piece // LANES), axis=1)
    for part in range(PARTS):
        arrived(partner.at[part], pair_recv.at[part], pair_send.at[0])
        mine = sums[PARTS + part].astype(jnp.float32)
        theirs = partner[part].astype(jnp.float32)
        conditional = jnp.where(first_branch, mine, theirs)
        unconditional = jnp.where(first_branch, theirs, mine)
        guided[:, part * piece : (part + 1) * piece] = (
            unconditional + wide * (conditional - unconditional)
        ).astype(jnp.bfloat16)
    for copy in sent:
        copy.wait_send()


def body(hidden, stale_kv, w_qkv, w_out, mod_table, segment_ids, step_index, guide_scale):
    rows, width = hidden.shape[1:]
    slab = stale_kv.shape[2]
    local = w_qkv.shape[2]
    heads = local // HEAD_DIM
    piece = width // 2 // PARTS
    bf16, f32 = jnp.bfloat16, jnp.float32
    anywhere = pl.BlockSpec(memory_space=pl.ANY)
    dma = pltpu.SemaphoreType.DMA
    def pinned(array):
        return pltpu.with_memory_space_constraint(array, pltpu.HBM)

    branch_rows, guided = pl.pallas_call(
        kernel,
        name="joint_attention",
        out_shape=(
            pltpu.VMEM((rows, width), bf16),
            pltpu.VMEM((rows, width // 2), bf16),
        ),
        in_specs=[anywhere] * 8,
        out_specs=(
            pl.BlockSpec(memory_space=pltpu.VMEM),
            pl.BlockSpec(memory_space=pltpu.VMEM),
        ),
        scratch_shapes=[
            pltpu.VMEM((rows, width), bf16),
            pltpu.VMEM((3, mod_table.shape[0], width), f32),
            pltpu.VMEM((NP, slab), jnp.int32),
            pltpu.SMEM(step_index.shape, jnp.int32),
            pltpu.SMEM(guide_scale.shape, f32),
            pltpu.VMEM((slab, slab), jnp.int32),
            pltpu.VMEM((3, width, local), bf16),
            pltpu.VMEM((local, width), bf16),
            pltpu.VMEM((slab, width), bf16),
            pltpu.VMEM((NZ, 2, slab, local), bf16),
            pltpu.VMEM((2, slab, local), bf16),
            pltpu.VMEM((slab, local), bf16),
            pltpu.VMEM((slab, local), bf16),
            pltpu.VMEM((2, slab, NZ * slab), f32),
            pltpu.VMEM((heads, slab, NZ * slab), f32),
            pltpu.VMEM((heads, slab, HEAD_DIM), bf16),
            pltpu.VMEM((heads, slab, HEAD_DIM), bf16),
            pltpu.VMEM((8, LANES), f32),
            pltpu.VMEM((8, LANES), f32),
            pltpu.VMEM((slab, local), bf16),
            pltpu.VMEM((2 * PARTS, slab, piece), bf16),
            pltpu.VMEM((2 * PARTS, 3, rows, piece), bf16),
            pltpu.VMEM((2 * PARTS, 3, rows, piece), bf16),
            pltpu.VMEM((2 * PARTS, 4, rows, piece), bf16),
            pltpu.VMEM((PARTS, rows, piece), bf16),
            dma((8,)),
            dma((7 * CHUNKS,)),
            dma((NZ, CHUNKS)),
            dma((2, 7)),
            dma((2, NT)),
            dma((2 + heads,)),
            dma((2 + heads,)),
            dma((2 * PARTS, NT - 1)),
            dma((2 * PARTS, NT - 1)),
            dma((PARTS,)),
            dma((PARTS,)),
        ],
        compiler_params=pltpu.CompilerParams(
            collective_id=0, has_side_effects=True, vmem_limit_bytes=48 << 20
        ),
    )(
        pinned(hidden[0]),
        pinned(stale_kv[0]),
        pinned(jnp.transpose(w_qkv, (1, 0, 2))),
        pinned(w_out),
        pinned(jnp.transpose(mod_table, (1, 0, 2))),
        pinned(segment_ids.reshape(NP, slab)),
        pinned(step_index),
        pinned(guide_scale),
    )
    return branch_rows[None], guided


def solution(mesh):
    placed = (
        P("cfg", ("patch", "tensor"), None),
        P("cfg", None, "patch", "tensor"),
        P(None, None, "tensor"),
        P("tensor", None),
        P(),
        P(),
        P(),
        P(),
    )
    return jax.shard_map(
        body,
        mesh=mesh,
        in_specs=placed,
        out_specs=(P("cfg", ("patch", "tensor"), None), P(("patch", "tensor"), "cfg")),
        check_vma=False,
    )
```

```python
import functools
import math

import jax
import jax.numpy as jnp
from jax import lax
from jax.experimental import pallas as pl
from jax.experimental.pallas import tpu as pltpu
from jax.sharding import PartitionSpec as P

MESH = pl.DeviceIdType.MESH
HEAD_DIM = 128
NZ = 8
NX = 4
NT = 8
NP = 16
KEY, VAL = 0, 1
NEG = -1e30


PARTS = 1
CHUNKS = 4
LANES = 128


def kernel(
    hidden,
    stale,
    w_qkv,
    w_out,
    mod_table,
    segments,
    step_index,
    guide_scale,
    branch,
    guided,
    hid,
    mods,
    segs,
    steps,
    strengths,
    query_segs,
    wq,
    wo,
    tokens,
    kv,
    fresh_kv,
    queries,
    far_queries,
    bias,
    scores,
    far_mixed,
    far_back,
    stats,
    stats_back,
    attn,
    partial,
    hops,
    onward,
    parts,
    partner,
    local_sem,
    kv_send,
    kv_recv,
    tok_send,
    tok_recv,
    far_send,
    far_recv,
    sum_send,
    sum_recv,
    pair_send,
    pair_recv,
):
    cfg = lax.axis_index("cfg")
    patch = lax.axis_index("patch")
    tensor = lax.axis_index("tensor")
    z, yh = patch // 2, patch % 2
    yl, x = tensor // NX, tensor % NX
    rows, width = hid.shape
    half = width // 2
    slab = queries.shape[0]
    heads = queries.shape[1] // HEAD_DIM
    chunk = 2 * slab // CHUNKS

    def tensor_peer(dx, dy):
        return (cfg, patch, ((yl + dy) % 2) * NX + (x + dx) % NX)

    up = (cfg, ((z + 1) % NZ) * 2 + yh, tensor)
    down = (cfg, ((z + NZ - 1) % NZ) * 2 + yh, tensor)
    across = (cfg, z * 2 + (1 - yh), tensor)
    core = (1 - cfg, patch, tensor)

    barrier = pltpu.get_barrier_semaphore()
    greeted = [up, down, across, core] + [tensor_peer(*to) for to in ((1, 0), (NX - 1, 0), (2, 0), (0, 1))]
    for device in greeted:
        pl.semaphore_signal(barrier, inc=1, device_id=device, device_id_type=MESH)

    loads = [
        pltpu.make_async_copy(hidden, hid, local_sem.at[0]),
        pltpu.make_async_copy(segments, segs, local_sem.at[1]),
        pltpu.make_async_copy(step_index, steps, local_sem.at[6]),
        pltpu.make_async_copy(guide_scale, strengths, local_sem.at[7]),
        pltpu.make_async_copy(mod_table, mods, local_sem.at[2]),
        pltpu.make_async_copy(w_qkv, wq, local_sem.at[3]),
        pltpu.make_async_copy(w_out, wo, local_sem.at[4]),
        pltpu.make_async_copy(stale, kv.at[0], local_sem.at[5]),
    ]
    for load in loads:
        load.start()

    sent = []

    def send(src, dst, send_sem, recv_sem, device):
        copy = pltpu.make_async_remote_copy(
            src_ref=src,
            dst_ref=dst,
            send_sem=send_sem,
            recv_sem=recv_sem,
            device_id=device,
            device_id_type=MESH,
        )
        copy.start()
        sent.append(copy)

    def arrived(dst, recv_sem, send_sem):
        pltpu.make_async_remote_copy(
            src_ref=dst,
            dst_ref=dst,
            send_sem=send_sem,
            recv_sem=recv_sem,
            device_id=core,
            device_id_type=MESH,
        ).wait_recv()

    counter = [0]

    def swap(c):
        return (c + CHUNKS // 2) % CHUNKS

    def block_of(ref, c):
        return ref.at[c // (CHUNKS // 2), pl.ds(c % (CHUNKS // 2) * chunk, chunk), :]

    def send_kv(src, d, c, device):
        send(
            src,
            block_of(kv.at[d % NZ], c),
            kv_send.at[counter[0]],
            kv_recv.at[d % NZ, c],
            device,
        )
        counter[0] += 1

    def take(d, c):
        here = block_of(kv.at[d % NZ], c)
        arrived(here, kv_recv.at[d % NZ, c], kv_send.at[0])
        if -3 < d < 0 or (d == -3 and c < CHUNKS // 2):
            send_kv(here, d - 1, c, up)
        if 0 < d < 3 or (d == 3 and c >= CHUNKS // 2):
            send_kv(here, d + 1, c, down)

    def token_block(dx, dy, part):
        at = (((yl + dy) % 2) * NX + (x + dx) % NX) * rows
        return tokens.at[pl.ds(pl.multiple_of(at, rows), rows), part * half : (part + 1) * half]

    def send_tokens(dx, dy, to_dx, to_dy, index, part):
        block = token_block(dx, dy, part)
        slot = ((dy + to_dy) % 2) * NX + (dx - to_dx) % NX
        send(
            block,
            block,
            tok_send.at[part, index],
            tok_recv.at[part, slot],
            tensor_peer(to_dx, to_dy),
        )

    def wait_tokens(dx, dy, part):
        arrived(token_block(dx, dy, part), tok_recv.at[part, dy * NX + dx], tok_send.at[0, 0])

    def relay_tokens(part):
        for index, dx in enumerate((1, NX - 1)):
            wait_tokens(dx, 0, part)
            send_tokens(dx, 0, 0, 1, 4 + index, part)
        wait_tokens(0, 1, part)
        send_tokens(0, 1, 2, 0, 6, part)

    pl.semaphore_wait(barrier, len(greeted))
    for c in range(CHUNKS):
        send_kv(block_of(stale, c), -1, c, up)
        send_kv(block_of(stale, swap(c)), 1, swap(c), down)

    loads[0].wait()
    residual = hid[...].astype(jnp.float32)
    mean = jnp.sum(residual, axis=-1, keepdims=True) * (1.0 / width)
    centred = residual - mean
    var = jnp.sum(centred * centred, axis=-1, keepdims=True) * (1.0 / width)
    normed = centred * lax.rsqrt(var + 1e-6)

    def column(which):
        row = segs[pl.ds(which, 1), :]
        return jnp.broadcast_to(row, (slab, slab)).T

    loads[1].wait()
    query_segs[...] = column(patch)
    own_segs = query_segs[pl.ds(pl.multiple_of(tensor * rows, rows), rows), :]
    for load in loads[2:5]:
        load.wait()

    def token_mods(which, start, count):
        wide = jnp.concatenate([own_segs] * (count // LANES), axis=1)
        picked = jnp.zeros((rows, count), jnp.float32)
        for r in range(8):
            row = mods[which, pl.ds(steps[r], 1), pl.ds(start, count)]
            picked = jnp.where(wide == r, row, picked)
        return picked

    own_rows = pl.ds(pl.multiple_of(tensor * rows, rows), rows)
    shift, scale = token_mods(0, 0, width), token_mods(1, 0, width)
    tokens[own_rows, :] = (normed * (1.0 + scale) + shift).astype(jnp.bfloat16)

    for part in range(2):
        send_tokens(0, 0, 1, 0, 0, part)
        send_tokens(0, 0, NX - 1, 0, 1, part)
        send_tokens(0, 0, 0, 1, 2, part)
    for part in range(2):
        send_tokens(0, 0, 2, 0, 3, part)

    def fill_bias(which, seg_column):
        for d in range(NZ):
            key_row = segs[pl.ds(((z + d) % NZ) * 2 + yh, 1), :]
            bias[which, :, d * slab : (d + 1) * slab] = jnp.where(seg_column == key_row, 0.0, NEG)

    def take_both(d, c):
        take(-d, c)
        take(d, swap(c))

    for c in range(CHUNKS // 2):
        take_both(1, c)
    relay_tokens(0)
    relay_tokens(1)
    for c in range(CHUNKS // 2, CHUNKS):
        take_both(1, c)
    fill_bias(0, query_segs[...])
    fill_bias(1, column(z * 2 + (1 - yh)))
    for c in range(CHUNKS):
        take_both(2, c)
    for part in range(2):
        for dx, dy in ((2, 0), (1, 1), (NX - 1, 1), (2, 1)):
            wait_tokens(dx, dy, part)
    loads[5].wait()
    queries[...] = jnp.dot(tokens[...], wq[0], preferred_element_type=jnp.float32).astype(
        jnp.bfloat16
    )
    send(queries, far_queries, far_send.at[0], far_recv.at[0], across)
    for c in range(CHUNKS):
        take_both(3, c)
    for j in (KEY, VAL):
        fresh_kv[j] = jnp.dot(
            tokens[...], wq[1 + j], preferred_element_type=jnp.float32
        ).astype(jnp.bfloat16)

    scale = math.log2(math.e) / HEAD_DIM**0.5

    def meet(which, q_ref, runs):
        cols = [slice(head * HEAD_DIM, (head + 1) * HEAD_DIM) for head in range(heads)]
        tops = []
        for head in range(heads):
            top = None
            for first, count in runs:
                at = slice(first * slab, (first + count) * slab)
                keys = kv[first : first + count, KEY, :, cols[head]].reshape(count * slab, HEAD_DIM)
                found = lax.dot_general(
                    q_ref[:, cols[head]],
                    keys,
                    (((1,), (1,)), ((), ())),
                    preferred_element_type=jnp.float32,
                )
                found = found * scale + bias[which, :, at]
                scores[head, :, at] = found
                for k in range(count):
                    piece = found[:, k * slab : (k + 1) * slab]
                    top = piece if top is None else jnp.maximum(top, piece)
            tops.append(jnp.max(top, axis=1, keepdims=True))
        met = []
        for head in range(heads):
            total, result = None, None
            for first, count in runs:
                at = slice(first * slab, (first + count) * slab)
                weights = jnp.exp2(scores[head, :, at] - tops[head])
                values = kv[first : first + count, VAL, :, cols[head]].reshape(
                    count * slab, HEAD_DIM
                )
                product = jnp.dot(
                    weights.astype(jnp.bfloat16), values, preferred_element_type=jnp.float32
                )
                result = product if result is None else result + product
                for k in range(count):
                    piece = weights[:, k * slab : (k + 1) * slab]
                    total = piece if total is None else total + piece
            met.append((tops[head], jnp.sum(total, axis=1, keepdims=True), result))
        return met

    def merge(one, two):
        top = jnp.maximum(one[0], two[0])
        left, right = jnp.exp2(one[0] - top), jnp.exp2(two[0] - top)
        return top, one[1] * left + two[1] * right, one[2] * left + two[2] * right

    early, late = ((0, 2), (2, 2), (5, 3)), ((4, 1),)

    arrived(far_queries, far_recv.at[0], far_send.at[0])
    loads[7].wait()
    far = meet(1, far_queries, early)
    for c in range(CHUNKS // 2):
        take(4, c)
        take(4, swap(c))
    lane = lax.broadcasted_iota(jnp.int32, (slab, LANES), 1)
    packed = jnp.zeros((slab, LANES), jnp.float32)
    far_late = meet(1, far_queries, late)
    for head in range(heads):
        top, total, result = merge(far[head], far_late[head])
        far_mixed[head] = result.astype(jnp.bfloat16)
        send(
            far_mixed.at[head],
            far_back.at[head],
            far_send.at[1 + head],
            far_recv.at[1 + head],
            across,
        )
        packed = jnp.where(lane == head, top, packed)
        packed = jnp.where(lane == heads + head, total, packed)
    stats[...] = packed.T[:8]
    send(stats, stats_back, far_send.at[1 + heads], far_recv.at[1 + heads], across)
    for j in (KEY, VAL):
        kv[0, j] = fresh_kv[j]
    own = meet(0, queries, ((0, 2), (2, 2), (4, 2), (6, 2)))

    arrived(stats_back, far_recv.at[1 + heads], far_send.at[0])
    back = jnp.concatenate([stats_back[...]] * (LANES // 8), axis=0).T
    for head in range(heads):
        cols = slice(head * HEAD_DIM, (head + 1) * HEAD_DIM)
        arrived(far_back.at[head], far_recv.at[1 + head], far_send.at[0])
        top, total, result = merge(
            own[head],
            (
                back[:, head : head + 1],
                back[:, heads + head : heads + head + 1],
                far_back[head].astype(jnp.float32),
            ),
        )
        attn[:, cols] = (result / total).astype(jnp.bfloat16)

    piece = half // PARTS
    starts = [
        pl.multiple_of(which * half + part * piece, piece)
        for which in (1 - cfg, cfg)
        for part in range(PARTS)
    ]
    loads[6].wait()

    def sum_rows(dx, dy):
        at = (((yl + dy) % 2) * NX + (x + dx) % NX) * rows
        return pl.ds(pl.multiple_of(at, rows), rows)

    for part in range(2 * PARTS):
        partial[part] = jnp.dot(
            attn[...], wo[:, pl.ds(starts[part], piece)], preferred_element_type=jnp.float32
        ).astype(jnp.bfloat16)
        for index, (row, to, landing) in enumerate(
            (
                (sum_rows(1, 1), tensor_peer(0, 1), hops.at[part, 0]),
                (sum_rows(NX - 1, 1), tensor_peer(0, 1), hops.at[part, 1]),
                (sum_rows(2, 1), tensor_peer(2, 0), hops.at[part, 2]),
                (sum_rows(2, 0), tensor_peer(2, 0), parts.at[part, 2]),
            )
        ):
            send(
                partial.at[part, row, :],
                landing,
                sum_send.at[part, index],
                sum_recv.at[part, index],
                to,
            )
    for copy in sent[:-8 * PARTS]:
        copy.wait_send()
    del sent[: -8 * PARTS]
    strength = jnp.zeros((rows, LANES), jnp.float32)
    for r in range(8):
        strength = jnp.where(own_segs == r, strengths[r], strength)
    gates = [token_mods(2, start, piece) for start in starts]

    for part in range(2 * PARTS):
        for index, (row, to, slot) in enumerate(
            (
                (sum_rows(1, 0), tensor_peer(1, 0), 0),
                (sum_rows(NX - 1, 0), tensor_peer(NX - 1, 0), 1),
                (sum_rows(0, 1), tensor_peer(0, 1), 3),
            )
        ):
            arrived(hops.at[part, index], sum_recv.at[part, index], sum_send.at[0, 0])
            both = hops[part, index].astype(jnp.float32) + partial[part, row, :].astype(jnp.float32)
            onward[part, index] = both.astype(jnp.bfloat16)
            send(
                onward.at[part, index],
                parts.at[part, slot],
                sum_send.at[part, 4 + index],
                sum_recv.at[part, 4 + index],
                to,
            )

    sums = []
    for part in range(2 * PARTS):
        cols = pl.ds(starts[part], piece)
        projected = partial[part, own_rows, :].astype(jnp.float32)
        for slot, sem in ((2, 3), (0, 4), (1, 5), (3, 6)):
            arrived(parts.at[part, slot], sum_recv.at[part, sem], sum_send.at[0, 0])
            projected = projected + parts[part, slot].astype(jnp.float32)
        total = hid[:, cols].astype(jnp.float32) + gates[part] * projected
        sums.append(total.astype(jnp.bfloat16))
        branch[:, cols] = sums[part]
        if part < PARTS:
            send(branch.at[:, cols], partner.at[part], pair_send.at[part], pair_recv.at[part], core)

    first_branch = cfg == 0
    wide = jnp.concatenate([strength] * (piece // LANES), axis=1)
    for part in range(PARTS):
        arrived(partner.at[part], pair_recv.at[part], pair_send.at[0])
        mine = sums[PARTS + part].astype(jnp.float32)
        theirs = partner[part].astype(jnp.float32)
        conditional = jnp.where(first_branch, mine, theirs)
        unconditional = jnp.where(first_branch, theirs, mine)
        guided[:, part * piece : (part + 1) * piece] = (
            unconditional + wide * (conditional - unconditional)
        ).astype(jnp.bfloat16)
    for copy in sent:
        copy.wait_send()


def body(hidden, stale_kv, w_qkv, w_out, mod_table, segment_ids, step_index, guide_scale):
    rows, width = hidden.shape[1:]
    slab = stale_kv.shape[2]
    local = w_qkv.shape[2]
    heads = local // HEAD_DIM
    piece = width // 2 // PARTS
    bf16, f32 = jnp.bfloat16, jnp.float32
    anywhere = pl.BlockSpec(memory_space=pl.ANY)
    dma = pltpu.SemaphoreType.DMA
    def pinned(array):
        return pltpu.with_memory_space_constraint(array, pltpu.HBM)

    branch_rows, guided = pl.pallas_call(
        kernel,
        name="joint_attention",
        out_shape=(
            pltpu.VMEM((rows, width), bf16),
            pltpu.VMEM((rows, width // 2), bf16),
        ),
        in_specs=[anywhere] * 8,
        out_specs=(
            pl.BlockSpec(memory_space=pltpu.VMEM),
            pl.BlockSpec(memory_space=pltpu.VMEM),
        ),
        scratch_shapes=[
            pltpu.VMEM((rows, width), bf16),
            pltpu.VMEM((3, mod_table.shape[0], width), f32),
            pltpu.VMEM((NP, slab), jnp.int32),
            pltpu.SMEM(step_index.shape, jnp.int32),
            pltpu.SMEM(guide_scale.shape, f32),
            pltpu.VMEM((slab, slab), jnp.int32),
            pltpu.VMEM((3, width, local), bf16),
            pltpu.VMEM((local, width), bf16),
            pltpu.VMEM((slab, width), bf16),
            pltpu.VMEM((NZ, 2, slab, local), bf16),
            pltpu.VMEM((2, slab, local), bf16),
            pltpu.VMEM((slab, local), bf16),
            pltpu.VMEM((slab, local), bf16),
            pltpu.VMEM((2, slab, NZ * slab), f32),
            pltpu.VMEM((heads, slab, NZ * slab), f32),
            pltpu.VMEM((heads, slab, HEAD_DIM), bf16),
            pltpu.VMEM((heads, slab, HEAD_DIM), bf16),
            pltpu.VMEM((8, LANES), f32),
            pltpu.VMEM((8, LANES), f32),
            pltpu.VMEM((slab, local), bf16),
            pltpu.VMEM((2 * PARTS, slab, piece), bf16),
            pltpu.VMEM((2 * PARTS, 3, rows, piece), bf16),
            pltpu.VMEM((2 * PARTS, 3, rows, piece), bf16),
            pltpu.VMEM((2 * PARTS, 4, rows, piece), bf16),
            pltpu.VMEM((PARTS, rows, piece), bf16),
            dma((8,)),
            dma((7 * CHUNKS,)),
            dma((NZ, CHUNKS)),
            dma((2, 7)),
            dma((2, NT)),
            dma((2 + heads,)),
            dma((2 + heads,)),
            dma((2 * PARTS, NT - 1)),
            dma((2 * PARTS, NT - 1)),
            dma((PARTS,)),
            dma((PARTS,)),
        ],
        compiler_params=pltpu.CompilerParams(
            collective_id=0, has_side_effects=True, vmem_limit_bytes=48 << 20
        ),
    )(
        pinned(hidden[0]),
        pinned(stale_kv[0]),
        pinned(jnp.transpose(w_qkv, (1, 0, 2))),
        pinned(w_out),
        pinned(jnp.transpose(mod_table, (1, 0, 2))),
        pinned(segment_ids.reshape(NP, slab)),
        pinned(step_index),
        pinned(guide_scale),
    )
    return branch_rows[None], guided


def solution(mesh):
    placed = (
        P("cfg", ("patch", "tensor"), None),
        P("cfg", None, "patch", "tensor"),
        P(None, None, "tensor"),
        P("tensor", None),
        P(),
        P(),
        P(),
        P(),
    )
    return jax.shard_map(
        body,
        mesh=mesh,
        in_specs=placed,
        out_specs=(P("cfg", ("patch", "tensor"), None), P(("patch", "tensor"), "cfg")),
        check_vma=False,
    )
```

```python
import functools
import math

import jax
import jax.numpy as jnp
from jax import lax
from jax.experimental import pallas as pl
from jax.experimental.pallas import tpu as pltpu
from jax.sharding import PartitionSpec as P

MESH = pl.DeviceIdType.MESH
HEAD_DIM = 128
NZ = 8
NX = 4
NT = 8
NP = 16
KEY, VAL = 0, 1
NEG = -1e30


PARTS = 1
CHUNKS = 4
LANES = 128


def kernel(
    hidden,
    stale,
    w_qkv,
    w_out,
    mod_table,
    segments,
    step_index,
    guide_scale,
    branch,
    guided,
    hid,
    mods,
    segs,
    steps,
    strengths,
    query_segs,
    wq,
    wo,
    tokens,
    kv,
    queries,
    far_queries,
    bias,
    scores,
    far_mixed,
    far_back,
    stats,
    stats_back,
    attn,
    partial,
    hops,
    onward,
    parts,
    partner,
    local_sem,
    kv_send,
    kv_recv,
    tok_send,
    tok_recv,
    far_send,
    far_recv,
    sum_send,
    sum_recv,
    pair_send,
    pair_recv,
):
    cfg = lax.axis_index("cfg")
    patch = lax.axis_index("patch")
    tensor = lax.axis_index("tensor")
    z, yh = patch // 2, patch % 2
    yl, x = tensor // NX, tensor % NX
    rows, width = hid.shape
    half = width // 2
    slab = queries.shape[0]
    heads = queries.shape[1] // HEAD_DIM
    chunk = 2 * slab // CHUNKS

    def tensor_peer(dx, dy):
        return (cfg, patch, ((yl + dy) % 2) * NX + (x + dx) % NX)

    up = (cfg, ((z + 1) % NZ) * 2 + yh, tensor)
    down = (cfg, ((z + NZ - 1) % NZ) * 2 + yh, tensor)
    across = (cfg, z * 2 + (1 - yh), tensor)
    core = (1 - cfg, patch, tensor)

    barrier = pltpu.get_barrier_semaphore()
    greeted = [up, down, across, core] + [tensor_peer(*to) for to in ((1, 0), (NX - 1, 0), (2, 0), (0, 1))]
    for device in greeted:
        pl.semaphore_signal(barrier, inc=1, device_id=device, device_id_type=MESH)

    loads = [
        pltpu.make_async_copy(hidden, hid, local_sem.at[0]),
        pltpu.make_async_copy(segments, segs, local_sem.at[1]),
        pltpu.make_async_copy(step_index, steps, local_sem.at[6]),
        pltpu.make_async_copy(guide_scale, strengths, local_sem.at[7]),
        pltpu.make_async_copy(mod_table, mods, local_sem.at[2]),
        pltpu.make_async_copy(w_qkv, wq, local_sem.at[3]),
        pltpu.make_async_copy(w_out, wo, local_sem.at[4]),
        pltpu.make_async_copy(stale, kv.at[0], local_sem.at[5]),
    ]
    for load in loads:
        load.start()

    sent = []

    def send(src, dst, send_sem, recv_sem, device):
        copy = pltpu.make_async_remote_copy(
            src_ref=src,
            dst_ref=dst,
            send_sem=send_sem,
            recv_sem=recv_sem,
            device_id=device,
            device_id_type=MESH,
        )
        copy.start()
        sent.append(copy)

    def arrived(dst, recv_sem, send_sem):
        pltpu.make_async_remote_copy(
            src_ref=dst,
            dst_ref=dst,
            send_sem=send_sem,
            recv_sem=recv_sem,
            device_id=core,
            device_id_type=MESH,
        ).wait_recv()

    counter = [0]

    def swap(c):
        return (c + CHUNKS // 2) % CHUNKS

    def block_of(ref, c):
        return ref.at[c // (CHUNKS // 2), pl.ds(c % (CHUNKS // 2) * chunk, chunk), :]

    def send_kv(src, d, c, device):
        send(
            src,
            block_of(kv.at[d % NZ], c),
            kv_send.at[counter[0]],
            kv_recv.at[d % NZ, c],
            device,
        )
        counter[0] += 1

    def take(d, c):
        here = block_of(kv.at[d % NZ], c)
        arrived(here, kv_recv.at[d % NZ, c], kv_send.at[0])
        if -3 < d < 0 or (d == -3 and c < CHUNKS // 2):
            send_kv(here, d - 1, c, up)
        if 0 < d < 3 or (d == 3 and c >= CHUNKS // 2):
            send_kv(here, d + 1, c, down)

    def token_block(dx, dy, part):
        at = (((yl + dy) % 2) * NX + (x + dx) % NX) * rows
        return tokens.at[pl.ds(pl.multiple_of(at, rows), rows), part * half : (part + 1) * half]

    def send_tokens(dx, dy, to_dx, to_dy, index, part):
        block = token_block(dx, dy, part)
        slot = ((dy + to_dy) % 2) * NX + (dx - to_dx) % NX
        send(
            block,
            block,
            tok_send.at[part, index],
            tok_recv.at[part, slot],
            tensor_peer(to_dx, to_dy),
        )

    def wait_tokens(dx, dy, part):
        arrived(token_block(dx, dy, part), tok_recv.at[part, dy * NX + dx], tok_send.at[0, 0])

    def relay_tokens(part):
        for index, dx in enumerate((1, NX - 1)):
            wait_tokens(dx, 0, part)
            send_tokens(dx, 0, 0, 1, 4 + index, part)
        wait_tokens(0, 1, part)
        send_tokens(0, 1, 2, 0, 6, part)

    pl.semaphore_wait(barrier, len(greeted))
    for c in range(CHUNKS):
        send_kv(block_of(stale, c), -1, c, up)
        send_kv(block_of(stale, swap(c)), 1, swap(c), down)

    loads[0].wait()
    residual = hid[...].astype(jnp.float32)
    mean = jnp.sum(residual, axis=-1, keepdims=True) * (1.0 / width)
    centred = residual - mean
    var = jnp.sum(centred * centred, axis=-1, keepdims=True) * (1.0 / width)
    normed = centred * lax.rsqrt(var + 1e-6)

    def column(which):
        row = segs[pl.ds(which, 1), :]
        return jnp.broadcast_to(row, (slab, slab)).T

    loads[1].wait()
    query_segs[...] = column(patch)
    own_segs = query_segs[pl.ds(pl.multiple_of(tensor * rows, rows), rows), :]
    for load in loads[2:5]:
        load.wait()

    def token_mods(which, start, count):
        wide = jnp.concatenate([own_segs] * (count // LANES), axis=1)
        picked = jnp.zeros((rows, count), jnp.float32)
        for r in range(8):
            row = mods[which, pl.ds(steps[r], 1), pl.ds(start, count)]
            picked = jnp.where(wide == r, row, picked)
        return picked

    own_rows = pl.ds(pl.multiple_of(tensor * rows, rows), rows)
    shift, scale = token_mods(0, 0, width), token_mods(1, 0, width)
    tokens[own_rows, :] = (normed * (1.0 + scale) + shift).astype(jnp.bfloat16)

    for part in range(2):
        send_tokens(0, 0, 1, 0, 0, part)
        send_tokens(0, 0, NX - 1, 0, 1, part)
        send_tokens(0, 0, 0, 1, 2, part)
    for part in range(2):
        send_tokens(0, 0, 2, 0, 3, part)

    def fill_bias(which, seg_column):
        for d in range(NZ):
            key_row = segs[pl.ds(((z + d) % NZ) * 2 + yh, 1), :]
            bias[which, :, d * slab : (d + 1) * slab] = jnp.where(seg_column == key_row, 0.0, NEG)

    def take_both(d, c):
        take(-d, c)
        take(d, swap(c))

    for c in range(CHUNKS // 2):
        take_both(1, c)
    relay_tokens(0)
    relay_tokens(1)
    for c in range(CHUNKS // 2, CHUNKS):
        take_both(1, c)
    fill_bias(0, query_segs[...])
    fill_bias(1, column(z * 2 + (1 - yh)))
    for c in range(CHUNKS):
        take_both(2, c)
    for part in range(2):
        for dx, dy in ((2, 0), (1, 1), (NX - 1, 1), (2, 1)):
            wait_tokens(dx, dy, part)
    loads[5].wait()
    queries[...] = jnp.dot(tokens[...], wq[0], preferred_element_type=jnp.float32).astype(
        jnp.bfloat16
    )
    send(queries, far_queries, far_send.at[0], far_recv.at[0], across)
    for c in range(CHUNKS):
        take_both(3, c)
    scale = math.log2(math.e) / HEAD_DIM**0.5

    def meet(which, q_ref, runs):
        cols = [slice(head * HEAD_DIM, (head + 1) * HEAD_DIM) for head in range(heads)]
        tops = []
        for head in range(heads):
            top = None
            for first, count in runs:
                at = slice(first * slab, (first + count) * slab)
                keys = kv[first : first + count, KEY, :, cols[head]].reshape(count * slab, HEAD_DIM)
                found = lax.dot_general(
                    q_ref[:, cols[head]],
                    keys,
                    (((1,), (1,)), ((), ())),
                    preferred_element_type=jnp.float32,
                )
                found = found * scale + bias[which, :, at]
                scores[head, :, at] = found
                for k in range(count):
                    piece = found[:, k * slab : (k + 1) * slab]
                    top = piece if top is None else jnp.maximum(top, piece)
            tops.append(jnp.max(top, axis=1, keepdims=True))
        met = []
        for head in range(heads):
            total, result = None, None
            for first, count in runs:
                at = slice(first * slab, (first + count) * slab)
                weights = jnp.exp2(scores[head, :, at] - tops[head])
                values = kv[first : first + count, VAL, :, cols[head]].reshape(
                    count * slab, HEAD_DIM
                )
                product = jnp.dot(
                    weights.astype(jnp.bfloat16), values, preferred_element_type=jnp.float32
                )
                result = product if result is None else result + product
                for k in range(count):
                    piece = weights[:, k * slab : (k + 1) * slab]
                    total = piece if total is None else total + piece
            met.append((tops[head], jnp.sum(total, axis=1, keepdims=True), result))
        return met

    def merge(one, two):
        top = jnp.maximum(one[0], two[0])
        left, right = jnp.exp2(one[0] - top), jnp.exp2(two[0] - top)
        return top, one[1] * left + two[1] * right, one[2] * left + two[2] * right

    early, late = ((0, 2), (2, 2), (5, 3)), ((4, 1),)

    arrived(far_queries, far_recv.at[0], far_send.at[0])
    loads[7].wait()
    far = meet(1, far_queries, early)
    for c in range(CHUNKS // 2):
        take(4, c)
        take(4, swap(c))
    lane = lax.broadcasted_iota(jnp.int32, (slab, LANES), 1)
    packed = jnp.zeros((slab, LANES), jnp.float32)
    far_late = meet(1, far_queries, late)
    for head in range(heads):
        top, total, result = merge(far[head], far_late[head])
        far_mixed[head] = result.astype(jnp.bfloat16)
        send(
            far_mixed.at[head],
            far_back.at[head],
            far_send.at[1 + head],
            far_recv.at[1 + head],
            across,
        )
        packed = jnp.where(lane == head, top, packed)
        packed = jnp.where(lane == heads + head, total, packed)
    stats[...] = packed.T[:8]
    send(stats, stats_back, far_send.at[1 + heads], far_recv.at[1 + heads], across)
    for j in (KEY, VAL):
        kv[0, j] = jnp.dot(
            tokens[...], wq[1 + j], preferred_element_type=jnp.float32
        ).astype(jnp.bfloat16)
    own = meet(0, queries, ((0, 2), (2, 2), (4, 2), (6, 2)))

    arrived(stats_back, far_recv.at[1 + heads], far_send.at[0])
    back = jnp.concatenate([stats_back[...]] * (LANES // 8), axis=0).T
    for head in range(heads):
        cols = slice(head * HEAD_DIM, (head + 1) * HEAD_DIM)
        arrived(far_back.at[head], far_recv.at[1 + head], far_send.at[0])
        top, total, result = merge(
            own[head],
            (
                back[:, head : head + 1],
                back[:, heads + head : heads + head + 1],
                far_back[head].astype(jnp.float32),
            ),
        )
        attn[:, cols] = (result / total).astype(jnp.bfloat16)

    piece = half // PARTS
    starts = [
        pl.multiple_of(which * half + part * piece, piece)
        for which in (1 - cfg, cfg)
        for part in range(PARTS)
    ]
    loads[6].wait()

    def sum_rows(dx, dy):
        at = (((yl + dy) % 2) * NX + (x + dx) % NX) * rows
        return pl.ds(pl.multiple_of(at, rows), rows)

    for part in range(2 * PARTS):
        partial[part] = jnp.dot(
            attn[...], wo[:, pl.ds(starts[part], piece)], preferred_element_type=jnp.float32
        ).astype(jnp.bfloat16)
        for index, (row, to, landing) in enumerate(
            (
                (sum_rows(1, 1), tensor_peer(0, 1), hops.at[part, 0]),
                (sum_rows(NX - 1, 1), tensor_peer(0, 1), hops.at[part, 1]),
                (sum_rows(2, 1), tensor_peer(2, 0), hops.at[part, 2]),
                (sum_rows(2, 0), tensor_peer(2, 0), parts.at[part, 2]),
            )
        ):
            send(
                partial.at[part, row, :],
                landing,
                sum_send.at[part, index],
                sum_recv.at[part, index],
                to,
            )
    for copy in sent[:-8 * PARTS]:
        copy.wait_send()
    del sent[: -8 * PARTS]
    strength = jnp.zeros((rows, LANES), jnp.float32)
    for r in range(8):
        strength = jnp.where(own_segs == r, strengths[r], strength)
    gates = [token_mods(2, start, piece) for start in starts]

    for part in range(2 * PARTS):
        for index, (row, to, slot) in enumerate(
            (
                (sum_rows(1, 0), tensor_peer(1, 0), 0),
                (sum_rows(NX - 1, 0), tensor_peer(NX - 1, 0), 1),
                (sum_rows(0, 1), tensor_peer(0, 1), 3),
            )
        ):
            arrived(hops.at[part, index], sum_recv.at[part, index], sum_send.at[0, 0])
            both = hops[part, index].astype(jnp.float32) + partial[part, row, :].astype(jnp.float32)
            onward[part, index] = both.astype(jnp.bfloat16)
            send(
                onward.at[part, index],
                parts.at[part, slot],
                sum_send.at[part, 4 + index],
                sum_recv.at[part, 4 + index],
                to,
            )

    sums = []
    for part in range(2 * PARTS):
        cols = pl.ds(starts[part], piece)
        projected = partial[part, own_rows, :].astype(jnp.float32)
        for slot, sem in ((2, 3), (0, 4), (1, 5), (3, 6)):
            arrived(parts.at[part, slot], sum_recv.at[part, sem], sum_send.at[0, 0])
            projected = projected + parts[part, slot].astype(jnp.float32)
        total = hid[:, cols].astype(jnp.float32) + gates[part] * projected
        sums.append(total.astype(jnp.bfloat16))
        branch[:, cols] = sums[part]
        if part < PARTS:
            send(branch.at[:, cols], partner.at[part], pair_send.at[part], pair_recv.at[part], core)

    first_branch = cfg == 0
    wide = jnp.concatenate([strength] * (piece // LANES), axis=1)
    for part in range(PARTS):
        arrived(partner.at[part], pair_recv.at[part], pair_send.at[0])
        mine = sums[PARTS + part].astype(jnp.float32)
        theirs = partner[part].astype(jnp.float32)
        conditional = jnp.where(first_branch, mine, theirs)
        unconditional = jnp.where(first_branch, theirs, mine)
        guided[:, part * piece : (part + 1) * piece] = (
            unconditional + wide * (conditional - unconditional)
        ).astype(jnp.bfloat16)
    for copy in sent:
        copy.wait_send()


def body(hidden, stale_kv, w_qkv, w_out, mod_table, segment_ids, step_index, guide_scale):
    rows, width = hidden.shape[1:]
    slab = stale_kv.shape[2]
    local = w_qkv.shape[2]
    heads = local // HEAD_DIM
    piece = width // 2 // PARTS
    bf16, f32 = jnp.bfloat16, jnp.float32
    anywhere = pl.BlockSpec(memory_space=pl.ANY)
    dma = pltpu.SemaphoreType.DMA
    def pinned(array):
        return pltpu.with_memory_space_constraint(array, pltpu.HBM)

    branch_rows, guided = pl.pallas_call(
        kernel,
        name="joint_attention",
        out_shape=(
            pltpu.VMEM((rows, width), bf16),
            pltpu.VMEM((rows, width // 2), bf16),
        ),
        in_specs=[anywhere] * 8,
        out_specs=(
            pl.BlockSpec(memory_space=pltpu.VMEM),
            pl.BlockSpec(memory_space=pltpu.VMEM),
        ),
        scratch_shapes=[
            pltpu.VMEM((rows, width), bf16),
            pltpu.VMEM((3, mod_table.shape[0], width), f32),
            pltpu.VMEM((NP, slab), jnp.int32),
            pltpu.SMEM(step_index.shape, jnp.int32),
            pltpu.SMEM(guide_scale.shape, f32),
            pltpu.VMEM((slab, slab), jnp.int32),
            pltpu.VMEM((3, width, local), bf16),
            pltpu.VMEM((local, width), bf16),
            pltpu.VMEM((slab, width), bf16),
            pltpu.VMEM((NZ, 2, slab, local), bf16),
            pltpu.VMEM((slab, local), bf16),
            pltpu.VMEM((slab, local), bf16),
            pltpu.VMEM((2, slab, NZ * slab), f32),
            pltpu.VMEM((heads, slab, NZ * slab), f32),
            pltpu.VMEM((heads, slab, HEAD_DIM), bf16),
            pltpu.VMEM((heads, slab, HEAD_DIM), bf16),
            pltpu.VMEM((8, LANES), f32),
            pltpu.VMEM((8, LANES), f32),
            pltpu.VMEM((slab, local), bf16),
            pltpu.VMEM((2 * PARTS, slab, piece), bf16),
            pltpu.VMEM((2 * PARTS, 3, rows, piece), bf16),
            pltpu.VMEM((2 * PARTS, 3, rows, piece), bf16),
            pltpu.VMEM((2 * PARTS, 4, rows, piece), bf16),
            pltpu.VMEM((PARTS, rows, piece), bf16),
            dma((8,)),
            dma((7 * CHUNKS,)),
            dma((NZ, CHUNKS)),
            dma((2, 7)),
            dma((2, NT)),
            dma((2 + heads,)),
            dma((2 + heads,)),
            dma((2 * PARTS, NT - 1)),
            dma((2 * PARTS, NT - 1)),
            dma((PARTS,)),
            dma((PARTS,)),
        ],
        compiler_params=pltpu.CompilerParams(
            collective_id=0, has_side_effects=True, vmem_limit_bytes=48 << 20
        ),
    )(
        pinned(hidden[0]),
        pinned(stale_kv[0]),
        pinned(jnp.transpose(w_qkv, (1, 0, 2))),
        pinned(w_out),
        pinned(jnp.transpose(mod_table, (1, 0, 2))),
        pinned(segment_ids.reshape(NP, slab)),
        pinned(step_index),
        pinned(guide_scale),
    )
    return branch_rows[None], guided


def solution(mesh):
    placed = (
        P("cfg", ("patch", "tensor"), None),
        P("cfg", None, "patch", "tensor"),
        P(None, None, "tensor"),
        P("tensor", None),
        P(),
        P(),
        P(),
        P(),
    )
    return jax.shard_map(
        body,
        mesh=mesh,
        in_specs=placed,
        out_specs=(P("cfg", ("patch", "tensor"), None), P(("patch", "tensor"), "cfg")),
        check_vma=False,
    )
```
